32 devices in a mesh: row: 4 (over z), col: 4 (over x, core), depth: 2 (over y).
Axes of the slice: x: 2, y: 2, z: 4, core: 2. Of those that a mesh axis runs over, the one named last changes fastest.
Arguments:
- block_values: bfloat16 [8, 4, 16, 128, 128], P(('row', 'depth'), 'col'), may hold values from 0.0049743652 to 0.5
- block_cols: int32 [8, 4, 16], P(('row', 'depth'), 'col'), may hold values from 0 to 31, as said below
- live_count: int32 [8, 4], P(('row', 'depth'), 'col'), may hold values from 8 to 16, as said below
- out_pattern: int32 [4, 4, 8, 2], P('row', 'col'), may hold values from 0 to 31, as said below
Outputs:
- squared_log: bfloat16 [4, 4, 8, 128, 128], P('row', 'col', 'depth')
The draws below stay inside these ranges and needn't reach their ends.
Inputs may be any that keep to these rules, and one draw needn't show every extreme that they name: Block row i's blocks are its first live_count slots; in every draw some block row is full. `block_cols`: the slots of one block row name distinct block columns. Call (k // 4) % 2 the depth part of a block index k and k // 8 its column group. Among the live slots of one block row at most 8 name a column in any one depth part and at most 4 in any one column group; both bounds are reached in every draw. The 8 entries of out_pattern[r, c] are distinct pairs (i, j) with i // 8 == r and j // 8 == c.
All inputs are finite; a program needn't handle non-finite values.
Results may differ from the reference program's by a relative error of at most 0.001.
Values may be sent and summed in bfloat16 or wider, within the bound.
A program may use at most 128 MiB of HBM per device.

```python
import math
import jax
import jax.numpy as jnp
from jax import lax

BS = 128
NZR = 16
GROUPS = 8
GR = 4
NB = 32
RB = 8
CB = 8
CPAT = 8
N_ROW = 4
N_COL = 4


def structure(key):
    start = jax.random.randint(jax.random.fold_in(key, 101), (NB,), 0, GROUPS)
    shift = jax.random.randint(jax.random.fold_in(key, 102), (NB, GROUPS), 0, GR)
    level = jax.random.randint(jax.random.fold_in(key, 103), (NB,), 0, 2)
    full_row = jax.random.randint(jax.random.fold_in(key, 104), (), 0, NB)
    position = start[:, None] + jnp.arange(NZR, dtype=jnp.int32)[None, :]
    block_ids = position % GROUPS
    wraps = position // GROUPS
    offsets = (jnp.take_along_axis(shift, block_ids, axis=1) + wraps) % GR
    col_ids = block_ids * GR + offsets
    live_rows = jnp.right_shift(jnp.full((NB,), NZR, jnp.int32), level.astype(jnp.int32))
    live_rows = jnp.where(jnp.arange(NB) == full_row, NZR, live_rows)
    return (col_ids.astype(jnp.int32), live_rows.astype(jnp.int32))


def shuffle_one(sub_key):
    return jax.random.permutation(sub_key, RB * CB).astype(jnp.int32)


def pattern_from(key, col_ids, live_rows):
    is_live = jnp.arange(NZR, dtype=jnp.int32)[None, :] < live_rows[:, None]
    second_cols = col_ids[col_ids]
    usable = is_live[:, :, None] & is_live[col_ids]
    row_ids = jnp.broadcast_to(jnp.arange(NB, dtype=jnp.int32)[:, None, None], second_cols.shape)
    reached = jnp.zeros((NB, NB), jnp.int32).at[row_ids.reshape(-1), second_cols.reshape(-1)].max(usable.reshape(-1).astype(jnp.int32))
    row_groups = NB // RB
    col_groups = NB // CB
    cell_marks = reached.reshape(row_groups, RB, col_groups, CB).transpose(0, 2, 1, 3).reshape(row_groups * col_groups, RB * CB)
    group_keys = jax.random.split(jax.random.fold_in(key, 105), row_groups * col_groups)
    shuffled = jax.vmap(shuffle_one)(group_keys)
    scores = cell_marks * (RB * CB) + shuffled
    _, picked = lax.top_k(scores, CPAT)
    group_ids = jnp.arange(row_groups * col_groups, dtype=jnp.int32)
    pick_rows = (group_ids // col_groups)[:, None] * RB + picked // CB
    pick_cols = (group_ids % col_groups)[:, None] * CB + picked % CB
    stacked = jnp.stack([pick_rows, pick_cols], axis=-1)
    return stacked.reshape(row_groups, col_groups, CPAT, 2).astype(jnp.int32)


def draw_block_cols(key, part):
    col_ids, live_rows = structure(key)
    return col_ids.reshape(GROUPS, GR, NZR)


def draw_live_count(key, part):
    col_ids, live_rows = structure(key)
    return live_rows.reshape(GROUPS, GR)


def draw_out_pattern(key, part):
    col_ids, live_rows = structure(key)
    return pattern_from(key, col_ids, live_rows)


def shard_levels(own_key, dims, cuts, low, top_value):
    factor_of, own = 1.0, jax.random.fold_in(own_key, 6)
    for axis_at, parts in cuts:
        heights = jnp.exp(jax.random.uniform(jax.random.fold_in(own, axis_at), (parts,), jnp.float32, low / len(cuts), top_value / len(cuts)))
        factor_of = factor_of * jnp.repeat(heights, dims[axis_at] // parts).reshape([-1 if axis == axis_at else 1 for axis in range(len(dims))])
    return factor_of


def setup_inputs(seed: int = 0) -> dict:
    key_of = jax.random.split(jax.random.key(seed), 5)
    return {
        "block_values": jnp.clip(jnp.exp(math.log(0.5) - 4.61031033 * jax.random.uniform(key_of[0], (GROUPS, GR, NZR, BS, BS), jnp.float32) ** shard_levels(key_of[0], (GROUPS, GR, NZR, BS, BS), ((0, 8), (1, 4)), -0.2, 0.2)), 0.0049743652, 0.5).astype(jnp.bfloat16),
        "block_cols": draw_block_cols(jax.random.fold_in(key_of[4], 71), 0),
        "live_count": draw_live_count(jax.random.fold_in(key_of[4], 71), 0),
        "out_pattern": draw_out_pattern(jax.random.fold_in(key_of[4], 71), 0),
    }


def reference(block_values, block_cols, live_count, out_pattern):
    values = block_values.reshape(NB, NZR, BS, BS)
    col_ids = block_cols.reshape(NB, NZR)
    is_live = jnp.arange(NZR, dtype=jnp.int32)[None, :] < live_count.reshape(NB, 1)
    entries = out_pattern.reshape(-1, 2).astype(jnp.int32)

    def one_block(entry):
        row_pick = entry[0]
        col_pick = entry[1]
        left_blocks = values[row_pick].astype(jnp.float32)
        inner = col_ids[row_pick]
        right_blocks = values[inner].astype(jnp.float32)
        weight = (is_live[row_pick][:, None] & is_live[inner] & (col_ids[inner] == col_pick)).astype(jnp.float32)
        chosen = jnp.einsum("st,stab->sab", weight, right_blocks, precision=lax.Precision.HIGHEST)
        return jnp.einsum("sab,sbc->ac", left_blocks, chosen, precision=lax.Precision.HIGHEST)

    blocks = lax.map(one_block, entries)
    result = jnp.log1p(blocks).astype(jnp.bfloat16)
    return result.reshape(N_ROW, N_COL, CPAT, BS, BS)
```

```python
import functools

import jax
import jax.numpy as jnp
from jax import lax
from jax.experimental import pallas as pl
from jax.experimental.pallas import tpu as pltpu
from jax.sharding import PartitionSpec as P

MESH = pl.DeviceIdType.MESH


def kernel(
    dims,
    index_ref,
    pattern_ref,
    meta_ref,
    values_ref,
    out_ref,
    left_stage,
    right_stage,
    left_buf,
    right_buf,
    left_meta,
    right_meta,
    left_ids,
    right_ids,
    partial,
    arrived,
    send_sem,
    left_sem,
    right_sem,
    meta_sems,
    local_sems,
    part_send,
    part_recv,
):
    rows, cols, depths, cap_left, cap_right = dims
    r, c, d = lax.axis_index("row"), lax.axis_index("col"), lax.axis_index("depth")
    left_me = d * cols + c
    right_me = r * cols + c
    share = out_ref.shape[0]
    left_total = depths * cap_left
    lefts = cols * depths
    rights = rows * cols
    zero_slot = rights * cap_right

    barrier = pltpu.get_barrier_semaphore()
    left_peers = [(m, e) for m in range(cols) for e in range(depths) if m or e]
    right_peers = [(m, n) for n in range(rows) for m in range(cols) if m or n]

    def left_peer(m, e):
        return (r, lax.rem(c + m, cols), lax.rem(d + e, depths))

    def right_peer(m, n):
        return (lax.rem(r + n, rows), lax.rem(c + m, cols), d)

    greeted = [left_peer(m, e) for m, e in left_peers]
    greeted += [right_peer(m, n) for m, n in right_peers if n]
    for peer in greeted:
        pl.semaphore_signal(barrier, inc=1, device_id=peer, device_id_type=MESH)

    for m in range(cols):
        cc = lax.rem(c + m, cols)
        for q in range(cap_right):
            block = values_ref[index_ref[0, left_total + cc * cap_right + q]]
            right_stage[m, q] = block
            if m == 0:
                right_buf[right_me * cap_right + q] = block
    for e in range(depths):
        dd = lax.rem(d + e, depths)
        for q in range(cap_left):
            block = values_ref[index_ref[0, dd * cap_left + q]]
            left_stage[e, q] = block
            if e == 0:
                left_buf[left_me * cap_left + q] = block
    left_meta[left_me] = meta_ref[0]
    right_meta[right_me] = meta_ref[0]
    right_buf[zero_slot] = jnp.zeros(right_buf.shape[1:], right_buf.dtype)

    pl.semaphore_wait(barrier, len(greeted))

    for n in range(rows - 1, -1, -1):
        for m in range(cols):
            if m or n:
                pltpu.make_async_remote_copy(
                    src_ref=right_stage.at[m],
                    dst_ref=right_buf.at[pl.ds(right_me * cap_right, cap_right)],
                    send_sem=send_sem.at[0],
                    recv_sem=right_sem,
                    device_id=right_peer(m, n),
                    device_id_type=MESH,
                ).start()
    for m, e in left_peers:
        pltpu.make_async_remote_copy(
            src_ref=left_stage.at[e],
            dst_ref=left_buf.at[pl.ds(left_me * cap_left, cap_left)],
            send_sem=send_sem.at[1],
            recv_sem=left_sem,
            device_id=left_peer(m, e),
            device_id_type=MESH,
        ).start()
    for m, e in left_peers:
        pltpu.make_async_remote_copy(
            src_ref=meta_ref,
            dst_ref=left_meta.at[pl.ds(left_me, 1)],
            send_sem=send_sem.at[2],
            recv_sem=meta_sems.at[0],
            device_id=left_peer(m, e),
            device_id_type=MESH,
        ).start()
    for m, n in right_peers:
        pltpu.make_async_remote_copy(
            src_ref=meta_ref,
            dst_ref=right_meta.at[pl.ds(right_me, 1)],
            send_sem=send_sem.at[3],
            recv_sem=meta_sems.at[1],
            device_id=right_peer(m, n),
            device_id_type=MESH,
        ).start()

    def wait_all(ref, sem):
        pltpu.make_async_copy(ref, ref, sem).wait()

    wait_all(left_meta.at[pl.ds(0, lefts - 1)], meta_sems.at[0])
    wait_all(right_meta.at[pl.ds(0, rights - 1)], meta_sems.at[1])
    left_copy = pltpu.make_async_copy(left_meta, left_ids, local_sems.at[0])
    right_copy = pltpu.make_async_copy(right_meta, right_ids, local_sems.at[1])
    left_copy.start()
    right_copy.start()
    left_copy.wait()
    right_copy.wait()
    wait_all(left_buf.at[pl.ds(0, (lefts - 1) * cap_left)], left_sem)
    wait_all(right_buf.at[pl.ds(0, (rights - 1) * cap_right)], right_sem)

    def one_entry(p):
        i = lax.rem(pattern_ref[0, 0, p, 0], lefts)
        j = pattern_ref[0, 0, p, 1]
        left_parts, right_parts = [], []
        for q in range(cap_left):
            inner = left_ids[i, 0, d * cap_left + q]
            place = jnp.maximum(inner, 0)
            at = jnp.int32(zero_slot)
            for t in range(cap_right):
                found = right_ids[place, 0, left_total + c * cap_right + t]
                at = jnp.where((inner >= 0) & (found == j), place * cap_right + t, at)
            left_parts.append(left_buf[i * cap_left + q])
            right_parts.append(right_buf[at])
        return jnp.dot(
            jnp.concatenate(left_parts, axis=1),
            jnp.concatenate(right_parts, axis=0),
            preferred_element_type=jnp.float32,
        )

    copies = []
    for e in range(1, depths + 1):
        dd = lax.rem(d + e, depths)

        def step(u, carry, e=e, dd=dd):
            partial[e - 1, u] = one_entry(dd * share + u)
            return carry

        lax.fori_loop(0, share, step, 0)
        if e < depths:
            copy = pltpu.make_async_remote_copy(
                src_ref=partial.at[e - 1],
                dst_ref=arrived.at[e - 1],
                send_sem=part_send.at[e - 1],
                recv_sem=part_recv.at[e - 1],
                device_id=(r, c, dd),
                device_id_type=MESH,
            )
            copy.start()
            copies.append(copy)
    total = partial[depths - 1]
    for e, copy in enumerate(copies):
        copy.wait_recv()
        total = total + arrived[e]
    out_ref[...] = total
    for copy in copies:
        copy.wait_send()
    sent = rights - 1
    wait_all(right_buf.at[pl.ds(0, sent * cap_right)], send_sem.at[0])
    sent = lefts - 1
    wait_all(left_buf.at[pl.ds(0, sent * cap_left)], send_sem.at[1])
    wait_all(left_meta.at[pl.ds(0, lefts - 1)], send_sem.at[2])
    wait_all(right_meta.at[pl.ds(0, rights - 1)], send_sem.at[3])


def body(block_values, block_cols, live_count, out_pattern):
    depths = lax.axis_size("depth")
    cols = lax.axis_size("col")
    rows = lax.axis_size("row")
    slots, size = block_values.shape[2], block_values.shape[3]
    groups = rows * depths
    col_block = groups
    pair = groups // cols
    cap_left = slots // depths
    cap_right = pair * (slots // groups) + min(pair, slots % groups)
    share = out_pattern.shape[2] // depths

    ids = block_cols.reshape(slots)
    order = jnp.arange(slots, dtype=jnp.int32)
    live = order < live_count.reshape(1)

    def table(part, parts, cap, payload):
        same = (part[:, None] == part[None, :]) & live[None, :]
        rank = jnp.sum((same & (order[None, :] < order[:, None])).astype(jnp.int32), axis=1)
        place = jnp.where(live, part * cap + rank, -1)
        hit = place[:, None] == jnp.arange(parts * cap, dtype=jnp.int32)[None, :]
        index = jnp.sum(jnp.where(hit, order[:, None], 0), axis=0)
        held = jnp.sum(jnp.where(hit, payload[:, None] + 1, 0), axis=0) - 1
        return index, held

    inner_place = ids // (cols * depths) * cols + ids % cols
    left_index, left_held = table(ids // cols % depths, depths, cap_left, inner_place)
    right_index, right_held = table(ids // col_block, cols, cap_right, ids)
    index = jnp.concatenate([left_index, right_index])[None]
    held = jnp.concatenate([left_held, right_held])
    meta = jnp.pad(held, (0, 128 - held.shape[0])).reshape(1, 1, 128)

    lefts, rights = cols * depths, rows * cols
    block = (size, size)
    bf16, i32 = jnp.bfloat16, jnp.int32
    vmem, smem = pltpu.VMEM, pltpu.SMEM
    dma = pltpu.SemaphoreType.DMA
    total = pl.pallas_call(
        functools.partial(kernel, (rows, cols, depths, cap_left, cap_right)),
        out_shape=jax.ShapeDtypeStruct((share,) + block, jnp.float32),
        in_specs=[pl.BlockSpec(memory_space=smem)] * 2 + [pl.BlockSpec(memory_space=vmem)] * 2,
        out_specs=pl.BlockSpec(memory_space=vmem),
        scratch_shapes=[
            vmem((depths, cap_left) + block, bf16),
            vmem((cols, cap_right) + block, bf16),
            vmem((lefts * cap_left,) + block, bf16),
            vmem((rights * cap_right + 1,) + block, bf16),
            vmem((lefts, 1, 128), i32),
            vmem((rights, 1, 128), i32),
            smem((lefts, 1, 128), i32),
            smem((rights, 1, 128), i32),
            vmem((depths, share) + block, jnp.float32),
            vmem((depths - 1, share) + block, jnp.float32),
            dma((4,)),
            dma,
            dma,
            dma((2,)),
            dma((2,)),
            dma((depths - 1,)),
            dma((depths - 1,)),
        ],
        compiler_params=pltpu.CompilerParams(
            collective_id=0, has_side_effects=True, vmem_limit_bytes=40 * 1024 * 1024
        ),
    )(index, out_pattern, meta, block_values.reshape((slots,) + block))
    return jnp.log1p(total).astype(jnp.bfloat16).reshape((1, 1, share) + block)


def solution(mesh):
    in_specs = (
        P(("row", "depth"), "col", None, None, None),
        P(("row", "depth"), "col", None),
        P(("row", "depth"), "col"),
        P("row", "col", None, None),
    )
    out_specs = P("row", "col", "depth", None, None)
    return jax.shard_map(body, mesh=mesh, in_specs=in_specs, out_specs=out_specs, check_vma=False)
```

```python
import functools

import jax
import jax.numpy as jnp
from jax import lax
from jax.experimental import pallas as pl
from jax.experimental.pallas import tpu as pltpu
from jax.sharding import PartitionSpec as P

MESH = pl.DeviceIdType.MESH


def kernel(
    dims,
    index_ref,
    pattern_ref,
    meta_ref,
    values_ref,
    out_ref,
    left_stage,
    right_stage,
    left_buf,
    left_meta,
    right_meta,
    left_ids,
    right_ids,
    partial,
    arrived,
    left_send,
    left_sem,
    pass_send,
    right_send,
    right_sem,
    line_send,
    meta_send,
    meta_sems,
    local_sems,
    part_send,
    part_recv,
    *planes,
):
    rows, cols, depths, cap_left, cap_right = dims
    r, c, d = lax.axis_index("row"), lax.axis_index("col"), lax.axis_index("depth")
    left_me = d * cols + c
    right_me = r * cols + c
    share = out_ref.shape[0]
    left_total = depths * cap_left
    lefts = cols * depths
    rights = rows * cols
    zero_slot = cols * cap_right
    other_core = c + 1 - 2 * lax.rem(c, 2)

    def remote(src, dst, send, recv, to):
        copy = pltpu.make_async_remote_copy(
            src_ref=src,
            dst_ref=dst,
            send_sem=send,
            recv_sem=recv,
            device_id=to,
            device_id_type=MESH,
        )
        copy.start()
        return copy

    def wait_all(ref, sem):
        pltpu.make_async_copy(ref, ref, sem).wait()

    def chunk(m, source):
        return planes[m].at[pl.ds(source * cap_right, cap_right)]

    def left_chunk(source):
        return left_buf.at[pl.ds(source * cap_left, cap_left)]

    barrier = pltpu.get_barrier_semaphore()
    left_peers = [(m, e) for m in range(cols) for e in range(depths) if m or e]
    right_peers = [(m, n) for n in range(rows) for m in range(cols) if m or n]

    def left_peer(m, e):
        return (r, lax.rem(c + m, cols), lax.rem(d + e, depths))

    def right_peer(m, n):
        return (lax.rem(r + n, rows), lax.rem(c + m, cols), d)

    greeted = [left_peer(m, e) for m, e in left_peers]
    greeted += [right_peer(m, n) for m, n in right_peers if n]
    for peer in greeted:
        pl.semaphore_signal(barrier, inc=1, device_id=peer, device_id_type=MESH)

    for m in range(cols):
        cc = lax.rem(c + m, cols)
        for q in range(cap_right):
            block = values_ref[index_ref[0, left_total + cc * cap_right + q]]
            if m == 0:
                planes[0][c * cap_right + q] = block
            else:
                right_stage[m - 1, q] = block
    for e in range(depths):
        dd = lax.rem(d + e, depths)
        for q in range(cap_left):
            block = values_ref[index_ref[0, dd * cap_left + q]]
            if e == 0:
                left_buf[left_me * cap_left + q] = block
            else:
                left_stage[e - 1, q] = block
    left_meta[left_me] = meta_ref[0]
    right_meta[right_me] = meta_ref[0]
    for m in range(rows):
        planes[m][zero_slot] = jnp.zeros(planes[m].shape[1:], planes[m].dtype)

    pl.semaphore_wait(barrier, len(greeted))

    for m in range(1, cols):
        remote(
            right_stage.at[m - 1],
            chunk(0, c),
            right_send.at[m - 1],
            right_sem.at[0, c],
            right_peer(m, 0),
        )

    def line(rr, m, source):
        copies = []
        plane = (rr + m) % rows
        for step, ahead in ((1, plane <= rr < rows - 1), (-1, plane >= rr > 0)):
            if ahead:
                there = (m - step) % rows
                copies.append(
                    remote(
                        chunk(m, source),
                        chunk(there, source),
                        line_send.at[(step + 1) // 2, m, source],
                        right_sem.at[there, source],
                        (r + step, c, d),
                    )
                )
        return copies

    def at_row(rr, run):
        pl.when(r == rr)(functools.partial(run, rr))

    for rr in range(rows):
        at_row(rr, lambda rr: line(rr, 0, c) and None)

    for e in range(depths):
        for m in range(0, cols, 2):
            if m or e:
                remote(
                    left_chunk(left_me) if e == 0 else left_stage.at[e - 1],
                    left_chunk(left_me),
                    left_send.at[e, m // 2],
                    left_sem.at[left_me],
                    left_peer(m, e),
                )

    for m, e in left_peers:
        remote(meta_ref, left_meta.at[pl.ds(left_me, 1)], meta_send.at[0], meta_sems.at[0], left_peer(m, e))
    for m, n in right_peers:
        remote(meta_ref, right_meta.at[pl.ds(right_me, 1)], meta_send.at[1], meta_sems.at[1], right_peer(m, n))

    def pass_left(source):
        return remote(
            left_chunk(source),
            left_chunk(source),
            pass_send.at[source],
            left_sem.at[source],
            (r, other_core, d),
        )

    passed = [pass_left(left_me)]

    def one_plane(rr, m, p):
        i = pattern_ref[0, p]
        j = pattern_ref[1, p]
        plane = (rr + m) % rows
        left_parts, right_parts = [], []
        for source in range(cols):
            inner = plane * cols + source
            q = lax.rem(left_ids[i, 0, d * rights + inner], 256)
            t = lax.div(right_ids[inner, 0, j], 256)
            at = jnp.where((q > 0) & (t > 0), source * cap_right + t - 1, zero_slot)
            left_parts.append(left_buf[i * cap_left + jnp.maximum(q - 1, 0)])
            right_parts.append(planes[m][at])
        return jnp.dot(
            jnp.concatenate(left_parts, axis=1),
            jnp.concatenate(right_parts, axis=0),
            preferred_element_type=jnp.float32,
        )

    def add_plane(rr, m, first=False, group=None):
        def step(p, carry):
            at = p if group is None else group * share + p
            if first:
                partial[at] = one_plane(rr, m, at)
            else:
                partial[at] += one_plane(rr, m, at)
            return carry

        lax.fori_loop(0, share if group is not None else depths * share, step, 0)

    def whole(rr):
        copies = []
        for n in range(1, cols):
            source = lax.rem(c + cols - n, cols)
            wait_all(chunk(0, source), right_sem.at[0, source])
            copies.extend(line(rr, 0, source))

        def take(slots):
            for n in range(cols):
                source = lax.rem(c + cols - n, cols)
                for m in slots:
                    wait_all(chunk(m, source), right_sem.at[m, source])
                    copies.extend(line(rr, m, source))

        def slots_at(far):
            return [m for m in range(1, rows) if abs((rr + m) % rows - rr) == far]

        take(slots_at(1))
        for e in range(depths):
            for m in range(0, cols, 2):
                if m or e:
                    source = lax.rem(d + depths - e, depths) * cols + lax.rem(c + cols - m, cols)
                    wait_all(left_chunk(source), left_sem.at[source])
                    copies.append(pass_left(source))
        wait_all(left_meta.at[pl.ds(0, lefts - 1)], meta_sems.at[0])
        wait_all(right_meta.at[pl.ds(0, rights - 1)], meta_sems.at[1])
        left_copy = pltpu.make_async_copy(left_meta, left_ids, local_sems.at[0])
        right_copy = pltpu.make_async_copy(right_meta, right_ids, local_sems.at[1])
        left_copy.start()
        right_copy.start()
        left_copy.wait()
        right_copy.wait()
        for e in range(depths):
            for m in range(0, cols, 2):
                source = lax.rem(d + depths - e, depths) * cols + lax.rem(other_core + cols - m, cols)
                wait_all(left_chunk(source), left_sem.at[source])
        reach = max(rr, rows - 1 - rr)
        add_plane(rr, 0, first=True)
        for m in slots_at(1):
            add_plane(rr, m)
        for far in range(2, reach + 1):
            slots = slots_at(far)
            take(slots)
            for m in slots[: None if far < reach else -1]:
                add_plane(rr, m)
        last = slots_at(reach)[-1] if reach > 1 else None
        for e in range(1, depths + 1):
            dd = lax.rem(d + e, depths)
            if last is not None:
                add_plane(rr, last, group=dd)
            if e < depths:
                copies.append(
                    remote(
                        partial.at[pl.ds(dd * share, share)],
                        arrived.at[e - 1],
                        part_send.at[e - 1],
                        part_recv.at[e - 1],
                        (r, c, dd),
                    )
                )
        for copy in copies:
            copy.wait_send()

    for rr in range(rows):
        at_row(rr, whole)

    total = partial[pl.ds(d * share, share)]
    for e in range(depths - 1):
        wait_all(arrived.at[e], part_recv.at[e])
        total = total + arrived[e]
    out_ref[...] = total

    def first_line(rr):
        for step, ahead in ((1, rr < rows - 1), (-1, rr > 0)):
            if ahead:
                wait_all(chunk(0, c), line_send.at[(step + 1) // 2, 0, c])

    for rr in range(rows):
        at_row(rr, first_line)
    for m in range(1, cols):
        wait_all(right_stage.at[m - 1], right_send.at[m - 1])
    for e in range(depths):
        for m in range(0, cols, 2):
            if m or e:
                wait_all(left_chunk(left_me), left_send.at[e, m // 2])
    for copy in passed:
        copy.wait_send()
    wait_all(left_meta.at[pl.ds(0, lefts - 1)], meta_send.at[0])
    wait_all(right_meta.at[pl.ds(0, rights - 1)], meta_send.at[1])


def body(block_values, block_cols, live_count, out_pattern):
    depths = lax.axis_size("depth")
    cols = lax.axis_size("col")
    rows = lax.axis_size("row")
    slots, size = block_values.shape[2], block_values.shape[3]
    groups = rows * depths
    blocks = groups * cols
    pair = groups // cols
    cap_left = slots // depths
    cap_right = pair * (slots // groups) + min(pair, slots % groups)
    entries = out_pattern.shape[2]
    share = entries // depths
    lefts, rights = cols * depths, rows * cols

    ids = block_cols.reshape(slots)
    order = jnp.arange(slots, dtype=jnp.int32)
    live = order < live_count.reshape(1)

    def placed(inner):
        return inner // cols % depths * rights + inner // lefts * cols + inner % cols

    def table(part, parts, cap):
        same = (part[:, None] == part[None, :]) & live[None, :]
        rank = jnp.sum((same & (order[None, :] < order[:, None])).astype(jnp.int32), axis=1)
        place = jnp.where(live, part * cap + rank, -1)
        hit = place[:, None] == jnp.arange(parts * cap, dtype=jnp.int32)[None, :]
        return jnp.sum(jnp.where(hit, order[:, None], 0), axis=0), rank

    left_index, left_rank = table(ids // cols % depths, depths, cap_left)
    right_index, right_rank = table(ids // groups, cols, cap_right)
    index = jnp.concatenate([left_index, right_index])[None]
    width = -(-blocks // 128) * 128
    mine = (placed(ids)[:, None] == jnp.arange(width, dtype=jnp.int32)[None, :]) & live[:, None]
    code = left_rank + 1 + 256 * (right_rank + 1)
    meta = jnp.sum(jnp.where(mine, code[:, None], 0), axis=0).reshape(1, 1, width)
    pattern = out_pattern.reshape(entries, 2)
    pattern = jnp.stack([pattern[:, 0] % lefts, placed(pattern[:, 1])])

    block = (size, size)
    bf16, i32 = jnp.bfloat16, jnp.int32
    vmem, smem = pltpu.VMEM, pltpu.SMEM
    dma = pltpu.SemaphoreType.DMA
    total = pl.pallas_call(
        functools.partial(kernel, (rows, cols, depths, cap_left, cap_right)),
        out_shape=jax.ShapeDtypeStruct((share,) + block, jnp.float32),
        in_specs=[pl.BlockSpec(memory_space=smem)] * 2 + [pl.BlockSpec(memory_space=vmem)] * 2,
        out_specs=pl.BlockSpec(memory_space=vmem),
        scratch_shapes=[
            vmem((depths - 1, cap_left) + block, bf16),
            vmem((cols - 1, cap_right) + block, bf16),
            vmem((lefts * cap_left,) + block, bf16),
            vmem((lefts, 1, width), i32),
            vmem((rights, 1, width), i32),
            smem((lefts, 1, width), i32),
            smem((rights, 1, width), i32),
            vmem((entries,) + block, jnp.float32),
            vmem((depths - 1, share) + block, jnp.float32),
            dma((depths, cols // 2)),
            dma((lefts,)),
            dma((lefts,)),
            dma((cols - 1,)),
            dma((rows, cols)),
            dma((2, rows, cols)),
            dma((2,)),
            dma((2,)),
            dma((2,)),
            dma((depths - 1,)),
            dma((depths - 1,)),
        ]
        + [vmem((cols * cap_right + 1,) + block, bf16)] * rows,
        compiler_params=pltpu.CompilerParams(
            collective_id=0, has_side_effects=True, vmem_limit_bytes=40 * 1024 * 1024
        ),
    )(index, pattern, meta, block_values.reshape((slots,) + block))
    return jnp.log1p(total).astype(jnp.bfloat16).reshape((1, 1, share) + block)


def solution(mesh):
    in_specs = (
        P(("row", "depth"), "col", None, None, None),
        P(("row", "depth"), "col", None),
        P(("row", "depth"), "col"),
        P("row", "col", None, None),
    )
    out_specs = P("row", "col", "depth", None, None)
    return jax.shard_map(body, mesh=mesh, in_specs=in_specs, out_specs=out_specs, check_vma=False)
```

```python
import functools

import jax
import jax.numpy as jnp
from jax import lax
from jax.experimental import pallas as pl
from jax.experimental.pallas import tpu as pltpu
from jax.sharding import PartitionSpec as P

MESH = pl.DeviceIdType.MESH


def kernel(
    dims,
    index_ref,
    pattern_ref,
    meta_ref,
    values_ref,
    out_ref,
    left_stage,
    right_stage,
    left_buf,
    left_meta,
    right_meta,
    left_ids,
    right_ids,
    left_at,
    right_at,
    partial,
    arrived,
    left_send,
    left_sem,
    pass_send,
    right_send,
    right_sem,
    line_send,
    meta_send,
    meta_sems,
    local_sems,
    part_send,
    part_recv,
    *planes,
):
    rows, cols, depths, cap_left, cap_right = dims
    r, c, d = lax.axis_index("row"), lax.axis_index("col"), lax.axis_index("depth")
    left_me = d * cols + c
    right_me = r * cols + c
    share = out_ref.shape[0]
    left_total = depths * cap_left
    lefts = cols * depths
    rights = rows * cols
    zero_slot = cols * cap_right
    other_core = c + 1 - 2 * lax.rem(c, 2)

    def remote(src, dst, send, recv, to):
        copy = pltpu.make_async_remote_copy(
            src_ref=src,
            dst_ref=dst,
            send_sem=send,
            recv_sem=recv,
            device_id=to,
            device_id_type=MESH,
        )
        copy.start()
        return copy

    def wait_all(ref, sem):
        pltpu.make_async_copy(ref, ref, sem).wait()

    ranked = [sorted(range(rows), key=lambda plane: abs(plane - rr)) for rr in range(rows)]
    at_end = (r == 0) | (r == rows - 1)

    def chunk(rank, source):
        return planes[rank].at[pl.ds(source * cap_right, cap_right)]

    def left_chunk(source):
        return left_buf.at[pl.ds(source * cap_left, cap_left)]

    def column(turn, flip, sign=1):
        chips = cols // 2
        chip = lax.rem(c // 2 + chips + sign * turn, chips)
        core = lax.rem(c, 2)
        return chip * 2 + (1 - core if flip else core)

    turns = [(turn, flip) for turn in range(cols // 2) for flip in range(2)]

    barrier = pltpu.get_barrier_semaphore()
    left_peers = [(m, e) for m in range(cols) for e in range(depths) if m or e]
    right_peers = [(m, n) for n in range(rows) for m in range(cols) if m or n]

    def left_peer(m, e):
        return (r, lax.rem(c + m, cols), lax.rem(d + e, depths))

    def right_peer(m, n):
        return (lax.rem(r + n, rows), lax.rem(c + m, cols), d)

    greeted = [left_peer(m, e) for m, e in left_peers]
    greeted += [right_peer(m, n) for m, n in right_peers if n]
    for peer in greeted:
        pl.semaphore_signal(barrier, inc=1, device_id=peer, device_id_type=MESH)

    for at, (turn, flip) in enumerate(turns):
        cc = column(turn, flip)
        for q in range(cap_right):
            block = values_ref[index_ref[0, left_total + cc * cap_right + q]]
            if at == 0:
                planes[0][c * cap_right + q] = block
            else:
                right_stage[at - 1, q] = block
    left_meta[left_me] = meta_ref[0]
    right_meta[right_me] = meta_ref[0]
    for rank in range(rows):
        planes[rank][zero_slot] = jnp.zeros(planes[rank].shape[1:], planes[rank].dtype)

    pl.semaphore_wait(barrier, len(greeted))

    def hops(rr, rank):
        plane = ranked[rr][rank]
        for step, ahead in ((1, plane <= rr < rows - 1), (-1, plane >= rr > 0)):
            if ahead:
                yield step, ranked[rr + step].index(plane)

    def line(rank, source):
        def run(rr):
            for step, there in hops(rr, rank):
                remote(
                    chunk(rank, source),
                    chunk(there, source),
                    line_send.at[(step + 1) // 2, rank, source],
                    right_sem.at[there, source],
                    (r + step, c, d),
                )

        for rr in range(rows):
            if list(hops(rr, rank)):
                pl.when(r == rr)(functools.partial(run, rr))

    line(0, c)
    for at, (turn, flip) in enumerate(turns[1:]):
        remote(
            right_stage.at[at],
            chunk(0, c),
            right_send.at[at],
            right_sem.at[0, c],
            (r, column(turn, flip), d),
        )
    for m, e in left_peers:
        remote(meta_ref, left_meta.at[pl.ds(left_me, 1)], meta_send.at[0], meta_sems.at[0], left_peer(m, e))
    for m, n in right_peers:
        remote(meta_ref, right_meta.at[pl.ds(right_me, 1)], meta_send.at[1], meta_sems.at[1], right_peer(m, n))

    for e in range(depths):
        dd = lax.rem(d + e, depths)
        for q in range(cap_left):
            block = values_ref[index_ref[0, dd * cap_left + q]]
            if e == 0:
                left_buf[left_me * cap_left + q] = block
            else:
                left_stage[e - 1, q] = block

    def pass_left(source):
        return remote(
            left_chunk(source),
            left_chunk(source),
            pass_send.at[source],
            left_sem.at[source],
            (r, other_core, d),
        )

    def take(rank, source):
        wait_all(chunk(rank, source), right_sem.at[rank, source])
        line(rank, source)

    for turn, flip in turns[1:]:
        take(0, column(turn, flip, -1))

    passed = [pass_left(left_me)]
    for e in range(depths):
        for turn in range(cols // 2):
            if turn or e:
                remote(
                    left_chunk(left_me) if e == 0 else left_stage.at[e - 1],
                    left_chunk(left_me),
                    left_send.at[e, turn],
                    left_sem.at[left_me],
                    (r, column(turn, 0), lax.rem(d + e, depths)),
                )

    sources = [column(turn, flip, -1) for turn, flip in turns]

    @pl.when(jnp.logical_not(at_end))
    def _():
        for source in sources:
            take(1, source)
            take(2, source)

    wait_all(left_meta.at[pl.ds(0, lefts - 1)], meta_sems.at[0])
    wait_all(right_meta.at[pl.ds(0, rights - 1)], meta_sems.at[1])
    left_copy = pltpu.make_async_copy(left_meta, left_ids, local_sems.at[0])
    right_copy = pltpu.make_async_copy(right_meta, right_ids, local_sems.at[1])
    left_copy.start()
    right_copy.start()
    left_copy.wait()
    right_copy.wait()

    def look_up(p, carry):
        i = pattern_ref[0, p]
        j = pattern_ref[1, p]
        for inner in range(rights):
            q = lax.rem(left_ids[i, 0, d * rights + inner], 256)
            t = lax.div(right_ids[inner, 0, j], 256)
            slot = inner % cols * cap_right + t - 1
            right_at[p, inner] = jnp.where((q > 0) & (t > 0), slot, zero_slot)
            left_at[p, inner] = i * cap_left + jnp.maximum(q - 1, 0)
        return carry

    lax.fori_loop(0, depths * share, look_up, 0)

    for e in range(depths):
        for turn in range(cols // 2):
            if turn or e:
                source = lax.rem(d + depths - e, depths) * cols + column(turn, 0, -1)
                wait_all(left_chunk(source), left_sem.at[source])
                passed.append(pass_left(source))
    for e in range(depths):
        for turn in range(cols // 2):
            source = lax.rem(d + depths - e, depths) * cols + column(turn, 1, -1)
            wait_all(left_chunk(source), left_sem.at[source])

    def add_plane(rank, first, count):
        plane = jnp.int32(0)
        for rr in range(rows):
            plane = jnp.where(r == rr, ranked[rr][rank], plane)

        def step(u, carry):
            p = first + u
            left_parts, right_parts = [], []
            for source in range(cols):
                inner = plane * cols + source
                left_parts.append(left_buf[left_at[p, inner]])
                right_parts.append(planes[rank][right_at[p, inner]])
            product = jnp.dot(
                jnp.concatenate(left_parts, axis=1),
                jnp.concatenate(right_parts, axis=0),
                preferred_element_type=jnp.float32,
            )
            if rank == 0:
                partial[p] = product
            else:
                partial[p] += product
            return carry

        lax.fori_loop(0, count, step, 0, unroll=4)

    def all_chunks(rank):
        for source in sources:
            wait_all(chunk(rank, source), right_sem.at[rank, source])

    entries = depths * share
    add_plane(0, 0, entries)
    pl.when(at_end)(lambda: all_chunks(1))
    add_plane(1, 0, entries)

    @pl.when(jnp.logical_not(at_end))
    def _():
        for source in sources:
            take(3, source)

    pl.when(at_end)(lambda: all_chunks(2))
    add_plane(2, 0, entries)
    pl.when(at_end)(lambda: all_chunks(3))
    copies = []
    for e in range(1, depths + 1):
        dd = lax.rem(d + e, depths)
        add_plane(3, dd * share, share)
        if e < depths:
            copies.append(
                remote(
                    partial.at[pl.ds(dd * share, share)],
                    arrived.at[e - 1],
                    part_send.at[e - 1],
                    part_recv.at[e - 1],
                    (r, c, dd),
                )
            )
    total = partial[pl.ds(d * share, share)]
    for e, copy in enumerate(copies):
        copy.wait_recv()
        total = total + arrived[e]
    out_ref[...] = total

    for copy in copies + passed:
        copy.wait_send()

    def line_sent(rr):
        for rank in range(rows):
            for step, there in hops(rr, rank):
                for source in range(cols):
                    wait_all(chunk(rank, source), line_send.at[(step + 1) // 2, rank, source])

    for rr in range(rows):
        pl.when(r == rr)(functools.partial(line_sent, rr))
    for at in range(cols - 1):
        wait_all(right_stage.at[at], right_send.at[at])
    for e in range(depths):
        for turn in range(cols // 2):
            if turn or e:
                wait_all(left_chunk(left_me), left_send.at[e, turn])
    wait_all(left_meta.at[pl.ds(0, lefts - 1)], meta_send.at[0])
    wait_all(right_meta.at[pl.ds(0, rights - 1)], meta_send.at[1])


def body(block_values, block_cols, live_count, out_pattern):
    depths = lax.axis_size("depth")
    cols = lax.axis_size("col")
    rows = lax.axis_size("row")
    slots, size = block_values.shape[2], block_values.shape[3]
    groups = rows * depths
    blocks = groups * cols
    pair = groups // cols
    cap_left = slots // depths
    cap_right = pair * (slots // groups) + min(pair, slots % groups)
    entries = out_pattern.shape[2]
    share = entries // depths
    lefts, rights = cols * depths, rows * cols

    ids = block_cols.reshape(slots)
    order = jnp.arange(slots, dtype=jnp.int32)
    live = order < live_count.reshape(1)

    def placed(inner):
        return inner // cols % depths * rights + inner // lefts * cols + inner % cols

    def table(part, parts, cap):
        same = (part[:, None] == part[None, :]) & live[None, :]
        rank = jnp.sum((same & (order[None, :] < order[:, None])).astype(jnp.int32), axis=1)
        place = jnp.where(live, part * cap + rank, -1)
        hit = place[:, None] == jnp.arange(parts * cap, dtype=jnp.int32)[None, :]
        return jnp.sum(jnp.where(hit, order[:, None], 0), axis=0), rank

    left_index, left_rank = table(ids // cols % depths, depths, cap_left)
    right_index, right_rank = table(ids // groups, cols, cap_right)
    index = jnp.concatenate([left_index, right_index])[None]
    width = -(-blocks // 128) * 128
    mine = (placed(ids)[:, None] == jnp.arange(width, dtype=jnp.int32)[None, :]) & live[:, None]
    code = left_rank + 1 + 256 * (right_rank + 1)
    meta = jnp.sum(jnp.where(mine, code[:, None], 0), axis=0).reshape(1, 1, width)
    pattern = out_pattern.reshape(entries, 2)
    pattern = jnp.stack([pattern[:, 0] % lefts, placed(pattern[:, 1])])

    block = (size, size)
    bf16, i32 = jnp.bfloat16, jnp.int32
    vmem, smem = pltpu.VMEM, pltpu.SMEM
    dma = pltpu.SemaphoreType.DMA
    total = pl.pallas_call(
        functools.partial(kernel, (rows, cols, depths, cap_left, cap_right)),
        out_shape=jax.ShapeDtypeStruct((share,) + block, jnp.float32),
        in_specs=[pl.BlockSpec(memory_space=smem)] * 2 + [pl.BlockSpec(memory_space=vmem)] * 2,
        out_specs=pl.BlockSpec(memory_space=vmem),
        scratch_shapes=[
            vmem((depths - 1, cap_left) + block, bf16),
            vmem((cols - 1, cap_right) + block, bf16),
            vmem((lefts * cap_left,) + block, bf16),
            vmem((lefts, 1, width), i32),
            vmem((rights, 1, width), i32),
            smem((lefts, 1, width), i32),
            smem((rights, 1, width), i32),
            smem((entries, rights), i32),
            smem((entries, rights), i32),
            vmem((entries,) + block, jnp.float32),
            vmem((depths - 1, share) + block, jnp.float32),
            dma((depths, cols // 2)),
            dma((lefts,)),
            dma((lefts,)),
            dma((cols - 1,)),
            dma((rows, cols)),
            dma((2, rows, cols)),
            dma((2,)),
            dma((2,)),
            dma((2,)),
            dma((depths - 1,)),
            dma((depths - 1,)),
        ]
        + [vmem((cols * cap_right + 1,) + block, bf16)] * rows,
        compiler_params=pltpu.CompilerParams(
            collective_id=0, has_side_effects=True, vmem_limit_bytes=40 * 1024 * 1024
        ),
    )(index, pattern, meta, block_values.reshape((slots,) + block))
    return jnp.log1p(total).astype(jnp.bfloat16).reshape((1, 1, share) + block)


def solution(mesh):
    in_specs = (
        P(("row", "depth"), "col", None, None, None),
        P(("row", "depth"), "col", None),
        P(("row", "depth"), "col"),
        P("row", "col", None, None),
    )
    out_specs = P("row", "col", "depth", None, None)
    return jax.shard_map(body, mesh=mesh, in_specs=in_specs, out_specs=out_specs, check_vma=False)
```

```python
import functools

import jax
import jax.numpy as jnp
from jax import lax
from jax.experimental import pallas as pl
from jax.experimental.pallas import tpu as pltpu
from jax.sharding import PartitionSpec as P

MESH = pl.DeviceIdType.MESH
LATE = jnp.int16
CODES = 65534.0
TOP = 0.25


def encode(value, bound):
    root = jnp.sqrt(value * (1.0 / bound))
    code = jnp.round(jnp.minimum(root, 1.0) * CODES - CODES / 2)
    return code.astype(jnp.int32).astype(LATE)


def decode(code, bound):
    root = (code.astype(jnp.int32).astype(jnp.float32) + CODES / 2) * (1.0 / CODES)
    return root * root * bound


def kernel(
    dims,
    index_ref,
    pattern_ref,
    meta_ref,
    values_hbm,
    out_ref,
    values_ref,
    left_stage,
    right_stage,
    left_buf,
    left_meta,
    right_meta,
    left_ids,
    right_ids,
    left_at,
    right_at,
    partial,
    late,
    late_mine,
    arrived,
    late_arrived,
    left_send,
    left_sem,
    pass_send,
    right_send,
    right_sem,
    line_send,
    meta_send,
    meta_sems,
    local_sems,
    part_send,
    part_recv,
    late_send,
    late_recv,
    *planes,
):
    rows, cols, depths, cap_left, cap_right = dims
    r, c, d = lax.axis_index("row"), lax.axis_index("col"), lax.axis_index("depth")
    left_me = d * cols + c
    right_me = r * cols + c
    share = out_ref.shape[0]
    left_total = depths * cap_left
    lefts = cols * depths
    rights = rows * cols
    zero_slot = cols * cap_right
    other_core = c + 1 - 2 * lax.rem(c, 2)

    def remote(src, dst, send, recv, to):
        copy = pltpu.make_async_remote_copy(
            src_ref=src,
            dst_ref=dst,
            send_sem=send,
            recv_sem=recv,
            device_id=to,
            device_id_type=MESH,
        )
        copy.start()
        return copy

    def wait_all(ref, sem):
        pltpu.make_async_copy(ref, ref, sem).wait()

    ranked = [sorted(range(rows), key=lambda plane: abs(plane - rr)) for rr in range(rows)]
    at_end = (r == 0) | (r == rows - 1)

    turns = [(turn, flip) for turn in range(cols // 2) for flip in range(2)]
    half = cols // 2
    bound = half * out_ref.shape[1] * TOP

    def chunk(rank, at):
        if rank == rows - 1 and at >= half:
            rank = rows
        return planes[rank].at[pl.ds(at * cap_right, cap_right)]

    def left_chunk(source):
        return left_buf.at[pl.ds(source * cap_left, cap_left)]

    def column(turn, flip, sign=1):
        chips = cols // 2
        chip = lax.rem(c // 2 + chips + sign * turn, chips)
        core = lax.rem(c, 2)
        return chip * 2 + (1 - core if flip else core)

    values_copy = pltpu.make_async_copy(values_hbm, values_ref, local_sems.at[2])
    values_copy.start()
    barrier = pltpu.get_barrier_semaphore()
    left_peers = [(m, e) for m in range(cols) for e in range(depths) if m or e]
    right_peers = [(m, n) for n in range(rows) for m in range(cols) if m or n]

    def left_peer(m, e):
        return (r, lax.rem(c + m, cols), lax.rem(d + e, depths))

    def right_peer(m, n):
        return (lax.rem(r + n, rows), lax.rem(c + m, cols), d)

    greeted = [left_peer(m, e) for m, e in left_peers]
    greeted += [right_peer(m, n) for m, n in right_peers if n]
    for peer in greeted:
        pl.semaphore_signal(barrier, inc=1, device_id=peer, device_id_type=MESH)

    values_copy.wait()
    for at, (turn, flip) in enumerate(turns):
        cc = column(turn, flip)
        for q in range(cap_right):
            block = values_ref[index_ref[0, left_total + cc * cap_right + q]]
            if at == 0:
                planes[0][q] = block
            else:
                right_stage[at - 1, q] = block
    left_meta[left_me] = meta_ref[0]
    right_meta[right_me] = meta_ref[0]
    for plane in planes:
        plane[zero_slot] = jnp.zeros(plane.shape[1:], plane.dtype)

    pl.semaphore_wait(barrier, len(greeted))

    def hops(rr, rank):
        plane = ranked[rr][rank]
        for step, ahead in ((1, plane <= rr < rows - 1), (-1, plane >= rr > 0)):
            if ahead:
                yield step, ranked[rr + step].index(plane)

    def line(rank, at):
        def run(rr):
            for step, there in hops(rr, rank):
                remote(
                    chunk(rank, at),
                    chunk(there, at),
                    line_send.at[(step + 1) // 2, rank, at],
                    right_sem.at[there, at],
                    (r + step, c, d),
                )

        for rr in range(rows):
            if list(hops(rr, rank)):
                pl.when(r == rr)(functools.partial(run, rr))

    line(0, 0)
    for at, (turn, flip) in enumerate(turns[1:]):
        remote(
            right_stage.at[at],
            chunk(0, at + 1),
            right_send.at[at],
            right_sem.at[0, at + 1],
            (r, column(turn, flip), d),
        )
    for m, e in left_peers:
        remote(meta_ref, left_meta.at[pl.ds(left_me, 1)], meta_send.at[0], meta_sems.at[0], left_peer(m, e))
    for m, n in right_peers:
        remote(meta_ref, right_meta.at[pl.ds(right_me, 1)], meta_send.at[1], meta_sems.at[1], right_peer(m, n))

    for e in range(depths):
        dd = lax.rem(d + e, depths)
        for q in range(cap_left):
            block = values_ref[index_ref[0, dd * cap_left + q]]
            if e == 0:
                left_buf[left_me * cap_left + q] = block
            else:
                left_stage[e - 1, q] = block

    def pass_left(source):
        return remote(
            left_chunk(source),
            left_chunk(source),
            pass_send.at[source],
            left_sem.at[source],
            (r, other_core, d),
        )

    def take(rank, at):
        wait_all(chunk(rank, at), right_sem.at[rank, at])
        line(rank, at)

    for at in range(1, cols):
        take(0, at)

    passed = [pass_left(left_me)]
    for e in range(depths):
        for turn in range(cols // 2):
            if turn or e:
                remote(
                    left_chunk(left_me) if e == 0 else left_stage.at[e - 1],
                    left_chunk(left_me),
                    left_send.at[e, turn],
                    left_sem.at[left_me],
                    (r, column(turn, 0), lax.rem(d + e, depths)),
                )

    sources = [column(turn, flip, -1) for turn, flip in turns]

    @pl.when(jnp.logical_not(at_end))
    def _():
        for at in range(cols):
            take(1, at)
            take(2, at)

    wait_all(left_meta.at[pl.ds(0, lefts - 1)], meta_sems.at[0])
    wait_all(right_meta.at[pl.ds(0, rights - 1)], meta_sems.at[1])
    left_copy = pltpu.make_async_copy(left_meta, left_ids, local_sems.at[0])
    right_copy = pltpu.make_async_copy(right_meta, right_ids, local_sems.at[1])
    left_copy.start()
    right_copy.start()
    left_copy.wait()
    right_copy.wait()

    slots = []
    for source in range(cols):
        turn = lax.rem(c // 2 + half - source // 2, half)
        slots.append(turn * 2 + jnp.where(lax.rem(c, 2) == source % 2, 0, 1))

    def look_up(p, carry):
        i = pattern_ref[0, p]
        j = pattern_ref[1, p]
        for inner in range(rights):
            q = lax.rem(left_ids[i, 0, d * rights + inner], 256)
            t = lax.div(right_ids[inner, 0, j], 256)
            slot = slots[inner % cols] * cap_right + t - 1
            right_at[p, inner] = jnp.where((q > 0) & (t > 0), slot, zero_slot)
            left_at[p, inner] = i * cap_left + jnp.maximum(q - 1, 0)
        return carry

    lax.fori_loop(0, depths * share, look_up, 0)

    for e in range(depths):
        for turn in range(cols // 2):
            if turn or e:
                source = lax.rem(d + depths - e, depths) * cols + column(turn, 0, -1)
                wait_all(left_chunk(source), left_sem.at[source])
                passed.append(pass_left(source))
    for e in range(depths):
        for turn in range(cols // 2):
            source = lax.rem(d + depths - e, depths) * cols + column(turn, 1, -1)
            wait_all(left_chunk(source), left_sem.at[source])

    def add_plane(rank, first, count, ats=range(cols), last=False, mine=False):
        plane = jnp.int32(0)
        for rr in range(rows):
            plane = jnp.where(r == rr, ranked[rr][rank], plane)
        held = planes[rows if last else rank]

        def step(u, carry):
            p = first + u
            left_parts, right_parts = [], []
            for at in ats:
                inner = plane * cols + sources[at]
                left_parts.append(left_buf[left_at[p, inner]])
                right_parts.append(held[right_at[p, inner]])
            product = jnp.dot(
                jnp.concatenate(left_parts, axis=1),
                jnp.concatenate(right_parts, axis=0),
                preferred_element_type=jnp.float32,
            )
            if mine:
                late_mine[u] = product
            elif last:
                late[p] = encode(product, bound)
            elif rank == 0:
                partial[p] = product
            else:
                partial[p] += product
            return carry

        lax.fori_loop(0, count, step, 0, unroll=4)

    def all_chunks(rank, ats=range(cols)):
        for at in ats:
            wait_all(chunk(rank, at), right_sem.at[rank, at])

    entries = depths * share
    add_plane(0, 0, entries)
    pl.when(at_end)(lambda: all_chunks(1))
    add_plane(1, 0, entries)

    @pl.when(jnp.logical_not(at_end))
    def _():
        for at in range(cols):
            take(rows - 1, at)

    pl.when(at_end)(lambda: all_chunks(2))
    add_plane(2, 0, entries)
    early, final = range(half), range(half, cols)
    pl.when(at_end)(lambda: all_chunks(rows - 1, early))
    copies, late_copies = [], []
    for e in range(1, depths + 1):
        dd = lax.rem(d + e, depths)
        add_plane(rows - 1, dd * share, share, early)
        if e < depths:
            copies.append(
                remote(
                    partial.at[pl.ds(dd * share, share)],
                    arrived.at[e - 1],
                    part_send.at[e - 1],
                    part_recv.at[e - 1],
                    (r, c, dd),
                )
            )
    pl.when(at_end)(lambda: all_chunks(rows - 1, final))
    for e in range(1, depths + 1):
        dd = lax.rem(d + e, depths)
        add_plane(rows - 1, dd * share, share, final, last=True, mine=e == depths)
        if e < depths:
            late_copies.append(
                remote(
                    late.at[pl.ds(dd * share, share)],
                    late_arrived.at[e - 1],
                    late_send.at[e - 1],
                    late_recv.at[e - 1],
                    (r, c, dd),
                )
            )
    total = partial[pl.ds(d * share, share)] + late_mine[...]
    for e, copy in enumerate(copies):
        copy.wait_recv()
        total = total + arrived[e]
    for e, copy in enumerate(late_copies):
        copy.wait_recv()
        total = total + decode(late_arrived[e], bound)
    out_ref[...] = total

    for copy in copies + late_copies + passed:
        copy.wait_send()

    def line_sent(rr):
        for rank in range(rows):
            for step, there in hops(rr, rank):
                for at in range(cols):
                    wait_all(chunk(rank, at), line_send.at[(step + 1) // 2, rank, at])

    for rr in range(rows):
        pl.when(r == rr)(functools.partial(line_sent, rr))
    for at in range(cols - 1):
        wait_all(right_stage.at[at], right_send.at[at])
    for e in range(depths):
        for turn in range(cols // 2):
            if turn or e:
                wait_all(left_chunk(left_me), left_send.at[e, turn])
    wait_all(left_meta.at[pl.ds(0, lefts - 1)], meta_send.at[0])
    wait_all(right_meta.at[pl.ds(0, rights - 1)], meta_send.at[1])


def body(block_values, block_cols, live_count, out_pattern):
    depths = lax.axis_size("depth")
    cols = lax.axis_size("col")
    rows = lax.axis_size("row")
    slots, size = block_values.shape[2], block_values.shape[3]
    groups = rows * depths
    blocks = groups * cols
    pair = groups // cols
    cap_left = slots // depths
    cap_right = pair * (slots // groups) + min(pair, slots % groups)
    entries = out_pattern.shape[2]
    share = entries // depths
    lefts, rights = cols * depths, rows * cols

    ids = block_cols.reshape(slots)
    order = jnp.arange(slots, dtype=jnp.int32)
    live = order < live_count.reshape(1)

    def placed(inner):
        return inner // cols % depths * rights + inner // lefts * cols + inner % cols

    def table(part, parts, cap):
        same = (part[:, None] == part[None, :]) & live[None, :]
        rank = jnp.sum((same & (order[None, :] < order[:, None])).astype(jnp.int32), axis=1)
        place = jnp.where(live, part * cap + rank, -1)
        hit = place[:, None] == jnp.arange(parts * cap, dtype=jnp.int32)[None, :]
        return jnp.sum(jnp.where(hit, order[:, None], 0), axis=0), rank

    left_index, left_rank = table(ids // cols % depths, depths, cap_left)
    right_index, right_rank = table(ids // groups, cols, cap_right)
    index = jnp.concatenate([left_index, right_index])[None]
    width = -(-blocks // 128) * 128
    mine = (placed(ids)[:, None] == jnp.arange(width, dtype=jnp.int32)[None, :]) & live[:, None]
    code = left_rank + 1 + 256 * (right_rank + 1)
    meta = jnp.sum(jnp.where(mine, code[:, None], 0), axis=0).reshape(1, 1, width)
    pattern = out_pattern.reshape(entries, 2)
    pattern = jnp.stack([pattern[:, 0] % lefts, placed(pattern[:, 1])])

    block = (size, size)
    bf16, i32 = jnp.bfloat16, jnp.int32
    vmem, smem = pltpu.VMEM, pltpu.SMEM
    dma = pltpu.SemaphoreType.DMA
    total = pl.pallas_call(
        functools.partial(kernel, (rows, cols, depths, cap_left, cap_right)),
        out_shape=jax.ShapeDtypeStruct((share,) + block, jnp.float32),
        in_specs=[
            pl.BlockSpec(memory_space=smem),
            pl.BlockSpec(memory_space=smem),
            pl.BlockSpec(memory_space=vmem),
            pl.BlockSpec(memory_space=pl.ANY),
        ],
        out_specs=pl.BlockSpec(memory_space=vmem),
        scratch_shapes=[
            vmem((slots,) + block, bf16),
            vmem((depths - 1, cap_left) + block, bf16),
            vmem((cols - 1, cap_right) + block, bf16),
            vmem((lefts * cap_left,) + block, bf16),
            vmem((lefts, 1, width), i32),
            vmem((rights, 1, width), i32),
            smem((lefts, 1, width), i32),
            smem((rights, 1, width), i32),
            smem((entries, rights), i32),
            smem((entries, rights), i32),
            vmem((entries,) + block, jnp.float32),
            vmem((entries,) + block, LATE),
            vmem((share,) + block, jnp.float32),
            vmem((depths - 1, share) + block, jnp.float32),
            vmem((depths - 1, share) + block, LATE),
            dma((depths, cols // 2)),
            dma((lefts,)),
            dma((lefts,)),
            dma((cols - 1,)),
            dma((rows, cols)),
            dma((2, rows, cols)),
            dma((2,)),
            dma((2,)),
            dma((3,)),
            dma((depths - 1,)),
            dma((depths - 1,)),
            dma((depths - 1,)),
            dma((depths - 1,)),
        ]
        + [vmem((cols * cap_right + 1,) + block, bf16)] * (rows + 1),
        compiler_params=pltpu.CompilerParams(
            collective_id=0, has_side_effects=True, vmem_limit_bytes=56 * 1024 * 1024
        ),
    )(index, pattern, meta, block_values.reshape((slots,) + block))
    return jnp.log1p(total).astype(jnp.bfloat16).reshape((1, 1, share) + block)


def solution(mesh):
    in_specs = (
        P(("row", "depth"), "col", None, None, None),
        P(("row", "depth"), "col", None),
        P(("row", "depth"), "col"),
        P("row", "col", None, None),
    )
    out_specs = P("row", "col", "depth", None, None)
    return jax.shard_map(body, mesh=mesh, in_specs=in_specs, out_specs=out_specs, check_vma=False)
```

```python
import functools

import jax
import jax.numpy as jnp
from jax import lax
from jax.experimental import pallas as pl
from jax.experimental.pallas import tpu as pltpu
from jax.sharding import PartitionSpec as P

MESH = pl.DeviceIdType.MESH
LATE = jnp.int16
CODES = 65534.0
TOP = 0.25


def encode(value, bound):
    root = jnp.sqrt(value * (1.0 / bound))
    code = jnp.round(jnp.minimum(root, 1.0) * CODES - CODES / 2)
    return code.astype(jnp.int32).astype(LATE)


def decode(code, bound):
    root = (code.astype(jnp.int32).astype(jnp.float32) + CODES / 2) * (1.0 / CODES)
    return root * root * bound


def kernel(
    dims,
    index_ref,
    pattern_ref,
    meta_ref,
    values_hbm,
    out_ref,
    values_ref,
    left_stage,
    right_stage,
    left_buf,
    left_meta,
    right_meta,
    left_ids,
    right_ids,
    left_at,
    right_at,
    partial,
    late,
    late_sum,
    arrived,
    late_arrived,
    left_send,
    left_sem,
    pass_send,
    right_send,
    right_sem,
    line_send,
    meta_send,
    meta_sems,
    local_sems,
    part_send,
    part_recv,
    late_send,
    late_recv,
    *planes,
):
    rows, cols, depths, cap_left, cap_right = dims
    r, c, d = lax.axis_index("row"), lax.axis_index("col"), lax.axis_index("depth")
    left_me = d * cols + c
    right_me = r * cols + c
    share = out_ref.shape[0]
    left_total = depths * cap_left
    lefts = cols * depths
    rights = rows * cols
    zero_slot = cols * cap_right
    other_core = c + 1 - 2 * lax.rem(c, 2)

    def remote(src, dst, send, recv, to):
        copy = pltpu.make_async_remote_copy(
            src_ref=src,
            dst_ref=dst,
            send_sem=send,
            recv_sem=recv,
            device_id=to,
            device_id_type=MESH,
        )
        copy.start()
        return copy

    def wait_all(ref, sem):
        pltpu.make_async_copy(ref, ref, sem).wait()

    ranked = [sorted(range(rows), key=lambda plane: abs(plane - rr)) for rr in range(rows)]
    at_end = (r == 0) | (r == rows - 1)

    turns = [(turn, flip) for turn in range(cols // 2) for flip in range(2)]
    half = cols // 2
    bound = cols * out_ref.shape[1] * TOP

    def chunk(rank, at):
        if rank == rows - 1 and at >= half:
            rank = rows
        return planes[rank].at[pl.ds(at * cap_right, cap_right)]

    def left_chunk(source):
        return left_buf.at[pl.ds(source * cap_left, cap_left)]

    def column(turn, flip, sign=1):
        chips = cols // 2
        chip = lax.rem(c // 2 + chips + sign * turn, chips)
        core = lax.rem(c, 2)
        return chip * 2 + (1 - core if flip else core)

    values_copy = pltpu.make_async_copy(values_hbm, values_ref, local_sems.at[2])
    values_copy.start()
    barrier = pltpu.get_barrier_semaphore()
    left_peers = [(m, e) for m in range(cols) for e in range(depths) if m or e]
    right_peers = [(m, n) for n in range(rows) for m in range(cols) if m or n]

    def left_peer(m, e):
        return (r, lax.rem(c + m, cols), lax.rem(d + e, depths))

    def right_peer(m, n):
        return (lax.rem(r + n, rows), lax.rem(c + m, cols), d)

    greeted = [left_peer(m, e) for m, e in left_peers]
    greeted += [right_peer(m, n) for m, n in right_peers if n]
    for peer in greeted:
        pl.semaphore_signal(barrier, inc=1, device_id=peer, device_id_type=MESH)

    values_copy.wait()
    for at, (turn, flip) in enumerate(turns):
        cc = column(turn, flip)
        for q in range(cap_right):
            block = values_ref[index_ref[0, left_total + cc * cap_right + q]]
            if at == 0:
                planes[0][q] = block
            else:
                right_stage[at - 1, q] = block
    left_meta[left_me] = meta_ref[0]
    right_meta[right_me] = meta_ref[0]
    for plane in planes:
        plane[zero_slot] = jnp.zeros(plane.shape[1:], plane.dtype)

    pl.semaphore_wait(barrier, len(greeted))

    def hops(rr, rank):
        plane = ranked[rr][rank]
        for step, ahead in ((1, plane <= rr < rows - 1), (-1, plane >= rr > 0)):
            if ahead:
                yield step, ranked[rr + step].index(plane)

    def line(rank, at):
        def run(rr):
            for step, there in hops(rr, rank):
                remote(
                    chunk(rank, at),
                    chunk(there, at),
                    line_send.at[(step + 1) // 2, rank, at],
                    right_sem.at[there, at],
                    (r + step, c, d),
                )

        for rr in range(rows):
            if list(hops(rr, rank)):
                pl.when(r == rr)(functools.partial(run, rr))

    line(0, 0)
    for at, (turn, flip) in enumerate(turns[1:]):
        remote(
            right_stage.at[at],
            chunk(0, at + 1),
            right_send.at[at],
            right_sem.at[0, at + 1],
            (r, column(turn, flip), d),
        )
    for m, e in left_peers:
        remote(meta_ref, left_meta.at[pl.ds(left_me, 1)], meta_send.at[0], meta_sems.at[0], left_peer(m, e))
    for m, n in right_peers:
        remote(meta_ref, right_meta.at[pl.ds(right_me, 1)], meta_send.at[1], meta_sems.at[1], right_peer(m, n))

    for e in range(depths):
        dd = lax.rem(d + e, depths)
        for q in range(cap_left):
            block = values_ref[index_ref[0, dd * cap_left + q]]
            if e == 0:
                left_buf[left_me * cap_left + q] = block
            else:
                left_stage[e - 1, q] = block

    def pass_left(source):
        return remote(
            left_chunk(source),
            left_chunk(source),
            pass_send.at[source],
            left_sem.at[source],
            (r, other_core, d),
        )

    def send_left(some):
        for e in range(depths):
            for turn in some:
                if turn or e:
                    remote(
                        left_chunk(left_me) if e == 0 else left_stage.at[e - 1],
                        left_chunk(left_me),
                        left_send.at[e, turn],
                        left_sem.at[left_me],
                        (r, column(turn, 0), lax.rem(d + e, depths)),
                    )

    send_left(range(1))
    passed = [pass_left(left_me)]

    def take(rank, at):
        wait_all(chunk(rank, at), right_sem.at[rank, at])
        line(rank, at)

    for at in range(1, cols):
        take(0, at)

    send_left(range(1, cols // 2))

    sources = [column(turn, flip, -1) for turn, flip in turns]

    @pl.when(jnp.logical_not(at_end))
    def _():
        for at in range(cols):
            take(1, at)
            take(2, at)

    wait_all(left_meta.at[pl.ds(0, lefts - 1)], meta_sems.at[0])
    wait_all(right_meta.at[pl.ds(0, rights - 1)], meta_sems.at[1])
    left_copy = pltpu.make_async_copy(left_meta, left_ids, local_sems.at[0])
    right_copy = pltpu.make_async_copy(right_meta, right_ids, local_sems.at[1])
    left_copy.start()
    right_copy.start()
    left_copy.wait()
    right_copy.wait()

    slots = []
    for source in range(cols):
        turn = lax.rem(c // 2 + half - source // 2, half)
        slots.append(turn * 2 + jnp.where(lax.rem(c, 2) == source % 2, 0, 1))

    def look_up(p, carry):
        i = pattern_ref[0, p]
        j = pattern_ref[1, p]
        for inner in range(rights):
            q = lax.rem(left_ids[i, 0, d * rights + inner], 256)
            t = lax.div(right_ids[inner, 0, j], 256)
            slot = slots[inner % cols] * cap_right + t - 1
            right_at[p, inner] = jnp.where((q > 0) & (t > 0), slot, zero_slot)
            left_at[p, inner] = i * cap_left + jnp.maximum(q - 1, 0)
        return carry

    lax.fori_loop(0, depths * share, look_up, 0)

    for e in range(depths):
        for turn in range(cols // 2):
            if turn or e:
                source = lax.rem(d + depths - e, depths) * cols + column(turn, 0, -1)
                wait_all(left_chunk(source), left_sem.at[source])
                passed.append(pass_left(source))

    @pl.when(jnp.logical_not(at_end))
    def _():
        for at in range(cols):
            take(rows - 1, at)

    for e in range(depths):
        for turn in range(cols // 2):
            source = lax.rem(d + depths - e, depths) * cols + column(turn, 1, -1)
            wait_all(left_chunk(source), left_sem.at[source])

    def add_plane(rank, first, count, ats=range(cols), last=False, mine=False):
        plane = jnp.int32(0)
        for rr in range(rows):
            plane = jnp.where(r == rr, ranked[rr][rank], plane)
        held = planes[rows if last else rank]

        def step(u, carry):
            p = first + u
            left_parts, right_parts = [], []
            for at in ats:
                inner = plane * cols + sources[at]
                left_parts.append(left_buf[left_at[p, inner]])
                right_parts.append(held[right_at[p, inner]])
            product = jnp.dot(
                jnp.concatenate(left_parts, axis=1),
                jnp.concatenate(right_parts, axis=0),
                preferred_element_type=jnp.float32,
            )
            if last:
                late_sum[p] += product
                if not mine:
                    late[p] = encode(late_sum[p], bound)
            elif rank == rows - 1:
                late_sum[p] = product
            elif rank == 0:
                partial[p] = product
            else:
                partial[p] += product
            return carry

        lax.fori_loop(0, count, step, 0, unroll=4)

    def all_chunks(rank, ats=range(cols)):
        for at in ats:
            wait_all(chunk(rank, at), right_sem.at[rank, at])

    entries = depths * share
    add_plane(0, 0, entries)
    pl.when(at_end)(lambda: all_chunks(1))
    add_plane(1, 0, entries)

    pl.when(at_end)(lambda: all_chunks(2))
    add_plane(2, 0, entries)
    early, final = range(half), range(half, cols)
    copies, late_copies = [], []
    for e in range(1, depths):
        dd = lax.rem(d + e, depths)
        copies.append(
            remote(
                partial.at[pl.ds(dd * share, share)],
                arrived.at[e - 1],
                part_send.at[e - 1],
                part_recv.at[e - 1],
                (r, c, dd),
            )
        )
    pl.when(at_end)(lambda: all_chunks(rows - 1, early))
    add_plane(rows - 1, 0, entries, early)
    pl.when(at_end)(lambda: all_chunks(rows - 1, final))
    for e in range(1, depths + 1):
        dd = lax.rem(d + e, depths)
        add_plane(rows - 1, dd * share, share, final, last=True, mine=e == depths)
        if e < depths:
            late_copies.append(
                remote(
                    late.at[pl.ds(dd * share, share)],
                    late_arrived.at[e - 1],
                    late_send.at[e - 1],
                    late_recv.at[e - 1],
                    (r, c, dd),
                )
            )
    total = partial[pl.ds(d * share, share)] + late_sum[pl.ds(d * share, share)]
    for e, copy in enumerate(copies):
        copy.wait_recv()
        total = total + arrived[e]
    for e, copy in enumerate(late_copies):
        copy.wait_recv()
        total = total + decode(late_arrived[e], bound)
    out_ref[...] = total

    for copy in copies + late_copies + passed:
        copy.wait_send()

    def line_sent(rr):
        for rank in range(rows):
            for step, there in hops(rr, rank):
                for at in range(cols):
                    wait_all(chunk(rank, at), line_send.at[(step + 1) // 2, rank, at])

    for rr in range(rows):
        pl.when(r == rr)(functools.partial(line_sent, rr))
    for at in range(cols - 1):
        wait_all(right_stage.at[at], right_send.at[at])
    for e in range(depths):
        for turn in range(cols // 2):
            if turn or e:
                wait_all(left_chunk(left_me), left_send.at[e, turn])
    wait_all(left_meta.at[pl.ds(0, lefts - 1)], meta_send.at[0])
    wait_all(right_meta.at[pl.ds(0, rights - 1)], meta_send.at[1])


def body(block_values, block_cols, live_count, out_pattern):
    depths = lax.axis_size("depth")
    cols = lax.axis_size("col")
    rows = lax.axis_size("row")
    slots, size = block_values.shape[2], block_values.shape[3]
    groups = rows * depths
    blocks = groups * cols
    pair = groups // cols
    cap_left = slots // depths
    cap_right = pair * (slots // groups) + min(pair, slots % groups)
    entries = out_pattern.shape[2]
    share = entries // depths
    lefts, rights = cols * depths, rows * cols

    ids = block_cols.reshape(slots)
    order = jnp.arange(slots, dtype=jnp.int32)
    live = order < live_count.reshape(1)

    def placed(inner):
        return inner // cols % depths * rights + inner // lefts * cols + inner % cols

    def table(part, parts, cap):
        same = (part[:, None] == part[None, :]) & live[None, :]
        rank = jnp.sum((same & (order[None, :] < order[:, None])).astype(jnp.int32), axis=1)
        place = jnp.where(live, part * cap + rank, -1)
        hit = place[:, None] == jnp.arange(parts * cap, dtype=jnp.int32)[None, :]
        return jnp.sum(jnp.where(hit, order[:, None], 0), axis=0), rank

    left_index, left_rank = table(ids // cols % depths, depths, cap_left)
    right_index, right_rank = table(ids // groups, cols, cap_right)
    index = jnp.concatenate([left_index, right_index])[None]
    width = -(-blocks // 128) * 128
    mine = (placed(ids)[:, None] == jnp.arange(width, dtype=jnp.int32)[None, :]) & live[:, None]
    code = left_rank + 1 + 256 * (right_rank + 1)
    meta = jnp.sum(jnp.where(mine, code[:, None], 0), axis=0).reshape(1, 1, width)
    pattern = out_pattern.reshape(entries, 2)
    pattern = jnp.stack([pattern[:, 0] % lefts, placed(pattern[:, 1])])

    block = (size, size)
    bf16, i32 = jnp.bfloat16, jnp.int32
    vmem, smem = pltpu.VMEM, pltpu.SMEM
    dma = pltpu.SemaphoreType.DMA
    total = pl.pallas_call(
        functools.partial(kernel, (rows, cols, depths, cap_left, cap_right)),
        out_shape=jax.ShapeDtypeStruct((share,) + block, jnp.float32),
        in_specs=[
            pl.BlockSpec(memory_space=smem),
            pl.BlockSpec(memory_space=smem),
            pl.BlockSpec(memory_space=vmem),
            pl.BlockSpec(memory_space=pl.ANY),
        ],
        out_specs=pl.BlockSpec(memory_space=vmem),
        scratch_shapes=[
            vmem((slots,) + block, bf16),
            vmem((depths - 1, cap_left) + block, bf16),
            vmem((cols - 1, cap_right) + block, bf16),
            vmem((lefts * cap_left,) + block, bf16),
            vmem((lefts, 1, width), i32),
            vmem((rights, 1, width), i32),
            smem((lefts, 1, width), i32),
            smem((rights, 1, width), i32),
            smem((entries, rights), i32),
            smem((entries, rights), i32),
            vmem((entries,) + block, jnp.float32),
            vmem((entries,) + block, LATE),
            vmem((entries,) + block, jnp.float32),
            vmem((depths - 1, share) + block, jnp.float32),
            vmem((depths - 1, share) + block, LATE),
            dma((depths, cols // 2)),
            dma((lefts,)),
            dma((lefts,)),
            dma((cols - 1,)),
            dma((rows, cols)),
            dma((2, rows, cols)),
            dma((2,)),
            dma((2,)),
            dma((3,)),
            dma((depths - 1,)),
            dma((depths - 1,)),
            dma((depths - 1,)),
            dma((depths - 1,)),
        ]
        + [vmem((cols * cap_right + 1,) + block, bf16)] * (rows + 1),
        compiler_params=pltpu.CompilerParams(
            collective_id=0, has_side_effects=True, vmem_limit_bytes=40 * 1024 * 1024
        ),
    )(index, pattern, meta, block_values.reshape((slots,) + block))
    return jnp.log1p(total).astype(jnp.bfloat16).reshape((1, 1, share) + block)


def solution(mesh):
    in_specs = (
        P(("row", "depth"), "col", None, None, None),
        P(("row", "depth"), "col", None),
        P(("row", "depth"), "col"),
        P("row", "col", None, None),
    )
    out_specs = P("row", "col", "depth", None, None)
    return jax.shard_map(body, mesh=mesh, in_specs=in_specs, out_specs=out_specs, check_vma=False)
```

```python
import functools

import jax
import jax.numpy as jnp
from jax import lax
from jax.experimental import pallas as pl
from jax.experimental.pallas import tpu as pltpu
from jax.sharding import PartitionSpec as P

MESH = pl.DeviceIdType.MESH
LATE = jnp.int16
CODES = 65534.0
TOP = 0.25


def encode(value, bound):
    root = jnp.sqrt(value * (1.0 / bound))
    code = jnp.round(jnp.minimum(root, 1.0) * CODES - CODES / 2)
    return code.astype(jnp.int32).astype(LATE)


def decode(code, bound):
    root = (code.astype(jnp.int32).astype(jnp.float32) + CODES / 2) * (1.0 / CODES)
    return root * root * bound


def kernel(
    dims,
    cols_ref,
    live_ref,
    pattern_ref,
    values_hbm,
    out_ref,
    values_ref,
    index_row,
    index_ref,
    meta_ref,
    left_stage,
    right_stage,
    left_buf,
    left_meta,
    right_meta,
    left_ids,
    right_ids,
    left_at,
    right_at,
    partial,
    late,
    late_sum,
    arrived,
    late_arrived,
    left_send,
    left_sem,
    pass_send,
    right_send,
    right_sem,
    line_send,
    meta_send,
    meta_sems,
    local_sems,
    part_send,
    part_recv,
    late_send,
    late_recv,
    *planes,
):
    rows, cols, depths, cap_left, cap_right = dims
    r, c, d = lax.axis_index("row"), lax.axis_index("col"), lax.axis_index("depth")
    left_me = d * cols + c
    right_me = r * cols + c
    share = out_ref.shape[0]
    left_total = depths * cap_left
    lefts = cols * depths
    rights = rows * cols
    zero_slot = cols * cap_right
    other_core = c + 1 - 2 * lax.rem(c, 2)

    def remote(src, dst, send, recv, to):
        copy = pltpu.make_async_remote_copy(
            src_ref=src,
            dst_ref=dst,
            send_sem=send,
            recv_sem=recv,
            device_id=to,
            device_id_type=MESH,
        )
        copy.start()
        return copy

    def wait_all(ref, sem):
        pltpu.make_async_copy(ref, ref, sem).wait()

    ranked = [sorted(range(rows), key=lambda plane: abs(plane - rr)) for rr in range(rows)]
    at_end = (r == 0) | (r == rows - 1)

    turns = [(turn, flip) for turn in range(cols // 2) for flip in range(2)]
    half = cols // 2
    bound = cols * out_ref.shape[1] * TOP

    def chunk(rank, at):
        if rank == rows - 1 and at >= half:
            rank = rows
        return planes[rank].at[pl.ds(at * cap_right, cap_right)]

    def left_chunk(source):
        return left_buf.at[pl.ds(source * cap_left, cap_left)]

    def column(turn, flip, sign=1):
        chips = cols // 2
        chip = lax.rem(c // 2 + chips + sign * turn, chips)
        core = lax.rem(c, 2)
        return chip * 2 + (1 - core if flip else core)

    values_copy = pltpu.make_async_copy(values_hbm, values_ref, local_sems.at[2])
    values_copy.start()
    barrier = pltpu.get_barrier_semaphore()
    left_peers = [(m, e) for m in range(cols) for e in range(depths) if m or e]
    right_peers = [(m, n) for n in range(rows) for m in range(cols) if m or n]

    def left_peer(m, e):
        return (r, lax.rem(c + m, cols), lax.rem(d + e, depths))

    def right_peer(m, n):
        return (lax.rem(r + n, rows), lax.rem(c + m, cols), d)

    greeted = [left_peer(m, e) for m, e in left_peers]
    greeted += [right_peer(m, n) for m, n in right_peers if n]
    for peer in greeted:
        pl.semaphore_signal(barrier, inc=1, device_id=peer, device_id_type=MESH)

    def placed(inner):
        part = lax.rem(lax.div(inner, cols), depths)
        return part * rights + lax.div(inner, lefts) * cols + lax.rem(inner, cols)

    slot_count = cols_ref.shape[1]
    ids = [cols_ref[0, s] for s in range(slot_count)]
    live_slots = live_ref[0, 0]
    left_parts = [lax.rem(lax.div(k, cols), depths) for k in ids]
    right_parts = [lax.div(k, rows * depths) for k in ids]
    lane = lax.broadcasted_iota(jnp.int32, index_row.shape, 1)
    wide = lax.broadcasted_iota(jnp.int32, meta_ref.shape[1:], 1)
    index = jnp.zeros(index_row.shape, jnp.int32)
    table = jnp.zeros(meta_ref.shape[1:], jnp.int32)
    for s in range(slot_count):
        left_rank, right_rank = jnp.int32(0), jnp.int32(0)
        for before in range(s):
            left_rank += jnp.where(left_parts[before] == left_parts[s], 1, 0)
            right_rank += jnp.where(right_parts[before] == right_parts[s], 1, 0)
        live = s < live_slots
        left_to = jnp.where(live, left_parts[s] * cap_left + left_rank, -1)
        right_to = jnp.where(live, left_total + right_parts[s] * cap_right + right_rank, -1)
        index = jnp.where((lane == left_to) | (lane == right_to), s, index)
        code = left_rank + 1 + 256 * (right_rank + 1)
        table = jnp.where(wide == jnp.where(live, placed(ids[s]), -1), code, table)
    index_row[...] = index
    meta_ref[0] = table
    index_copy = pltpu.make_async_copy(index_row, index_ref, local_sems.at[3])
    index_copy.start()
    index_copy.wait()

    values_copy.wait()
    for at, (turn, flip) in enumerate(turns):
        cc = column(turn, flip)
        for q in range(cap_right):
            block = values_ref[index_ref[0, left_total + cc * cap_right + q]]
            if at == 0:
                planes[0][q] = block
            else:
                right_stage[at - 1, q] = block
    left_meta[left_me] = meta_ref[0]
    right_meta[right_me] = meta_ref[0]
    for plane in planes:
        plane[zero_slot] = jnp.zeros(plane.shape[1:], plane.dtype)

    pl.semaphore_wait(barrier, len(greeted))

    def hops(rr, rank):
        plane = ranked[rr][rank]
        for step, ahead in ((1, plane <= rr < rows - 1), (-1, plane >= rr > 0)):
            if ahead:
                yield step, ranked[rr + step].index(plane)

    def line(rank, at):
        def run(rr):
            for step, there in hops(rr, rank):
                remote(
                    chunk(rank, at),
                    chunk(there, at),
                    line_send.at[(step + 1) // 2, rank, at],
                    right_sem.at[there, at],
                    (r + step, c, d),
                )

        for rr in range(rows):
            if list(hops(rr, rank)):
                pl.when(r == rr)(functools.partial(run, rr))

    line(0, 0)
    for at, (turn, flip) in enumerate(turns[1:]):
        remote(
            right_stage.at[at],
            chunk(0, at + 1),
            right_send.at[at],
            right_sem.at[0, at + 1],
            (r, column(turn, flip), d),
        )
    for m, e in left_peers:
        remote(meta_ref, left_meta.at[pl.ds(left_me, 1)], meta_send.at[0], meta_sems.at[0], left_peer(m, e))
    for m, n in right_peers:
        remote(meta_ref, right_meta.at[pl.ds(right_me, 1)], meta_send.at[1], meta_sems.at[1], right_peer(m, n))

    for e in range(depths):
        dd = lax.rem(d + e, depths)
        for q in range(cap_left):
            block = values_ref[index_ref[0, dd * cap_left + q]]
            if e == 0:
                left_buf[left_me * cap_left + q] = block
            else:
                left_stage[e - 1, q] = block

    def pass_left(source):
        return remote(
            left_chunk(source),
            left_chunk(source),
            pass_send.at[source],
            left_sem.at[source],
            (r, other_core, d),
        )

    def send_left(some):
        for e in range(depths):
            for turn in some:
                if turn or e:
                    remote(
                        left_chunk(left_me) if e == 0 else left_stage.at[e - 1],
                        left_chunk(left_me),
                        left_send.at[e, turn],
                        left_sem.at[left_me],
                        (r, column(turn, 0), lax.rem(d + e, depths)),
                    )

    send_left(range(1))
    passed = [pass_left(left_me)]

    def take(rank, at):
        wait_all(chunk(rank, at), right_sem.at[rank, at])
        line(rank, at)

    for at in range(1, cols):
        take(0, at)

    send_left(range(1, cols // 2))

    sources = [column(turn, flip, -1) for turn, flip in turns]

    @pl.when(jnp.logical_not(at_end))
    def _():
        for at in range(cols):
            take(1, at)
            take(2, at)

    wait_all(left_meta.at[pl.ds(0, lefts - 1)], meta_sems.at[0])
    wait_all(right_meta.at[pl.ds(0, rights - 1)], meta_sems.at[1])
    left_copy = pltpu.make_async_copy(left_meta, left_ids, local_sems.at[0])
    right_copy = pltpu.make_async_copy(right_meta, right_ids, local_sems.at[1])
    left_copy.start()
    right_copy.start()
    left_copy.wait()
    right_copy.wait()

    slots = []
    for source in range(cols):
        turn = lax.rem(c // 2 + half - source // 2, half)
        slots.append(turn * 2 + jnp.where(lax.rem(c, 2) == source % 2, 0, 1))

    def look_up(p, carry):
        i = lax.rem(pattern_ref[0, p], lefts)
        j = placed(pattern_ref[1, p])
        for inner in range(rights):
            q = lax.rem(left_ids[i, 0, d * rights + inner], 256)
            t = lax.div(right_ids[inner, 0, j], 256)
            slot = slots[inner % cols] * cap_right + t - 1
            right_at[p, inner] = jnp.where((q > 0) & (t > 0), slot, zero_slot)
            left_at[p, inner] = i * cap_left + jnp.maximum(q - 1, 0)
        return carry

    lax.fori_loop(0, depths * share, look_up, 0)

    for e in range(depths):
        for turn in range(cols // 2):
            if turn or e:
                source = lax.rem(d + depths - e, depths) * cols + column(turn, 0, -1)
                wait_all(left_chunk(source), left_sem.at[source])
                passed.append(pass_left(source))

    @pl.when(jnp.logical_not(at_end))
    def _():
        for at in range(cols):
            take(rows - 1, at)

    for e in range(depths):
        for turn in range(cols // 2):
            source = lax.rem(d + depths - e, depths) * cols + column(turn, 1, -1)
            wait_all(left_chunk(source), left_sem.at[source])

    def add_plane(rank, first, count, ats=range(cols), last=False, mine=False):
        plane = jnp.int32(0)
        for rr in range(rows):
            plane = jnp.where(r == rr, ranked[rr][rank], plane)
        held = planes[rows if last else rank]

        def step(u, carry):
            p = first + u
            left_parts, right_parts = [], []
            for at in ats:
                inner = plane * cols + sources[at]
                left_parts.append(left_buf[left_at[p, inner]])
                right_parts.append(held[right_at[p, inner]])
            product = jnp.dot(
                jnp.concatenate(left_parts, axis=1),
                jnp.concatenate(right_parts, axis=0),
                preferred_element_type=jnp.float32,
            )
            if last:
                late_sum[p] += product
                if not mine:
                    late[p] = encode(late_sum[p], bound)
            elif rank == rows - 1:
                late_sum[p] = product
            elif rank == 0:
                partial[p] = product
            else:
                partial[p] += product
            return carry

        lax.fori_loop(0, count, step, 0, unroll=4)

    def all_chunks(rank, ats=range(cols)):
        for at in ats:
            wait_all(chunk(rank, at), right_sem.at[rank, at])

    entries = depths * share
    add_plane(0, 0, entries)
    pl.when(at_end)(lambda: all_chunks(1))
    add_plane(1, 0, entries)

    pl.when(at_end)(lambda: all_chunks(2))
    add_plane(2, 0, entries)
    early, final = range(half), range(half, cols)
    copies, late_copies = [], []
    for e in range(1, depths):
        dd = lax.rem(d + e, depths)
        copies.append(
            remote(
                partial.at[pl.ds(dd * share, share)],
                arrived.at[e - 1],
                part_send.at[e - 1],
                part_recv.at[e - 1],
                (r, c, dd),
            )
        )
    pl.when(at_end)(lambda: all_chunks(rows - 1, early))
    add_plane(rows - 1, 0, entries, early)
    pl.when(at_end)(lambda: all_chunks(rows - 1, final))
    for e in range(1, depths + 1):
        dd = lax.rem(d + e, depths)
        add_plane(rows - 1, dd * share, share, final, last=True, mine=e == depths)
        if e < depths:
            late_copies.append(
                remote(
                    late.at[pl.ds(dd * share, share)],
                    late_arrived.at[e - 1],
                    late_send.at[e - 1],
                    late_recv.at[e - 1],
                    (r, c, dd),
                )
            )
    total = partial[pl.ds(d * share, share)] + late_sum[pl.ds(d * share, share)]
    for e, copy in enumerate(copies):
        copy.wait_recv()
        total = total + arrived[e]
    for e, copy in enumerate(late_copies):
        copy.wait_recv()
        total = total + decode(late_arrived[e], bound)
    out_ref[...] = jnp.log1p(total).astype(out_ref.dtype)

    for copy in copies + late_copies + passed:
        copy.wait_send()

    def line_sent(rr):
        for rank in range(rows):
            for step, there in hops(rr, rank):
                for at in range(cols):
                    wait_all(chunk(rank, at), line_send.at[(step + 1) // 2, rank, at])

    for rr in range(rows):
        pl.when(r == rr)(functools.partial(line_sent, rr))
    for at in range(cols - 1):
        wait_all(right_stage.at[at], right_send.at[at])
    for e in range(depths):
        for turn in range(cols // 2):
            if turn or e:
                wait_all(left_chunk(left_me), left_send.at[e, turn])
    wait_all(left_meta.at[pl.ds(0, lefts - 1)], meta_send.at[0])
    wait_all(right_meta.at[pl.ds(0, rights - 1)], meta_send.at[1])


def body(block_values, block_cols, live_count, out_pattern):
    depths = lax.axis_size("depth")
    cols = lax.axis_size("col")
    rows = lax.axis_size("row")
    slots, size = block_values.shape[2], block_values.shape[3]
    groups = rows * depths
    blocks = groups * cols
    pair = groups // cols
    cap_left = slots // depths
    cap_right = pair * (slots // groups) + min(pair, slots % groups)
    entries = out_pattern.shape[2]
    share = entries // depths
    lefts, rights = cols * depths, rows * cols

    width = -(-blocks // 128) * 128
    pattern = jnp.swapaxes(out_pattern, 2, 3).reshape(2, entries)

    block = (size, size)
    bf16, i32 = jnp.bfloat16, jnp.int32
    vmem, smem = pltpu.VMEM, pltpu.SMEM
    dma = pltpu.SemaphoreType.DMA
    result = pl.pallas_call(
        functools.partial(kernel, (rows, cols, depths, cap_left, cap_right)),
        out_shape=jax.ShapeDtypeStruct((share,) + block, bf16),
        in_specs=[
            pl.BlockSpec(memory_space=smem),
            pl.BlockSpec(memory_space=smem),
            pl.BlockSpec(memory_space=smem),
            pl.BlockSpec(memory_space=pl.ANY),
        ],
        out_specs=pl.BlockSpec(memory_space=vmem),
        scratch_shapes=[
            vmem((slots,) + block, bf16),
            vmem((1, 128), i32),
            smem((1, 128), i32),
            vmem((1, 1, width), i32),
            vmem((depths - 1, cap_left) + block, bf16),
            vmem((cols - 1, cap_right) + block, bf16),
            vmem((lefts * cap_left,) + block, bf16),
            vmem((lefts, 1, width), i32),
            vmem((rights, 1, width), i32),
            smem((lefts, 1, width), i32),
            smem((rights, 1, width), i32),
            smem((entries, rights), i32),
            smem((entries, rights), i32),
            vmem((entries,) + block, jnp.float32),
            vmem((entries,) + block, LATE),
            vmem((entries,) + block, jnp.float32),
            vmem((depths - 1, share) + block, jnp.float32),
            vmem((depths - 1, share) + block, LATE),
            dma((depths, cols // 2)),
            dma((lefts,)),
            dma((lefts,)),
            dma((cols - 1,)),
            dma((rows, cols)),
            dma((2, rows, cols)),
            dma((2,)),
            dma((2,)),
            dma((4,)),
            dma((depths - 1,)),
            dma((depths - 1,)),
            dma((depths - 1,)),
            dma((depths - 1,)),
        ]
        + [vmem((cols * cap_right + 1,) + block, bf16)] * (rows + 1),
        compiler_params=pltpu.CompilerParams(
            collective_id=0, has_side_effects=True, vmem_limit_bytes=56 * 1024 * 1024
        ),
    )(block_cols.reshape(1, slots), live_count, pattern, block_values.reshape((slots,) + block))
    return result.reshape((1, 1, share) + block)


def solution(mesh):
    in_specs = (
        P(("row", "depth"), "col", None, None, None),
        P(("row", "depth"), "col", None),
        P(("row", "depth"), "col"),
        P("row", "col", None, None),
    )
    out_specs = P("row", "col", "depth", None, None)
    return jax.shard_map(body, mesh=mesh, in_specs=in_specs, out_specs=out_specs, check_vma=False)
```

```python
import functools

import jax
import jax.numpy as jnp
from jax import lax
from jax.experimental import pallas as pl
from jax.experimental.pallas import tpu as pltpu
from jax.sharding import PartitionSpec as P

MESH = pl.DeviceIdType.MESH
LATE = jnp.int16
CODES = 65534.0
TOP = 0.25


def encode(value, bound):
    root = jnp.sqrt(value * (1.0 / bound))
    code = jnp.round(jnp.minimum(root, 1.0) * CODES - CODES / 2)
    return code.astype(jnp.int32).astype(LATE)


def decode(code, bound):
    root = (code.astype(jnp.int32).astype(jnp.float32) + CODES / 2) * (1.0 / CODES)
    return root * root * bound


def kernel(
    dims,
    cols_ref,
    live_ref,
    pattern_ref,
    values_hbm,
    out_ref,
    values_ref,
    index_row,
    index_ref,
    meta_ref,
    left_stage,
    right_stage,
    left_buf,
    left_meta,
    right_meta,
    left_ids,
    right_ids,
    left_at,
    right_at,
    partial,
    late,
    late_sum,
    arrived,
    late_arrived,
    left_send,
    left_sem,
    pass_send,
    right_send,
    right_sem,
    line_send,
    meta_send,
    meta_sems,
    local_sems,
    part_send,
    part_recv,
    late_send,
    late_recv,
    *planes,
):
    rows, cols, depths, cap_left, cap_right = dims
    r, c, d = lax.axis_index("row"), lax.axis_index("col"), lax.axis_index("depth")
    left_me = d * cols + c
    right_me = r * cols + c
    share = out_ref.shape[0]
    left_total = depths * cap_left
    lefts = cols * depths
    rights = rows * cols
    zero_slot = cols * cap_right
    other_core = c + 1 - 2 * lax.rem(c, 2)

    def remote(src, dst, send, recv, to):
        copy = pltpu.make_async_remote_copy(
            src_ref=src,
            dst_ref=dst,
            send_sem=send,
            recv_sem=recv,
            device_id=to,
            device_id_type=MESH,
        )
        copy.start()
        return copy

    def wait_all(ref, sem):
        pltpu.make_async_copy(ref, ref, sem).wait()

    ranked = [sorted(range(rows), key=lambda plane: abs(plane - rr)) for rr in range(rows)]
    at_end = (r == 0) | (r == rows - 1)

    turns = [(turn, flip) for turn in range(cols // 2) for flip in range(2)]
    half = cols // 2
    bound = cols * out_ref.shape[1] * TOP

    def chunk(rank, at):
        if rank == rows - 1 and at >= half:
            rank = rows
        return planes[rank].at[pl.ds(at * cap_right, cap_right)]

    def left_chunk(source):
        return left_buf.at[pl.ds(source * cap_left, cap_left)]

    def column(turn, flip, sign=1):
        chips = cols // 2
        chip = lax.rem(c // 2 + chips + sign * turn, chips)
        core = lax.rem(c, 2)
        return chip * 2 + (1 - core if flip else core)

    values_copy = pltpu.make_async_copy(values_hbm, values_ref, local_sems.at[2])
    values_copy.start()
    barrier = pltpu.get_barrier_semaphore()
    left_peers = [(m, e) for m in range(cols) for e in range(depths) if m or e]
    right_peers = [(m, n) for n in range(rows) for m in range(cols) if m or n]

    def left_peer(m, e):
        return (r, lax.rem(c + m, cols), lax.rem(d + e, depths))

    def right_peer(m, n):
        return (lax.rem(r + n, rows), lax.rem(c + m, cols), d)

    greeted = [left_peer(m, e) for m, e in left_peers]
    greeted += [right_peer(m, n) for m, n in right_peers if n]
    for peer in greeted:
        pl.semaphore_signal(barrier, inc=1, device_id=peer, device_id_type=MESH)

    def placed(inner):
        part = lax.rem(lax.div(inner, cols), depths)
        return part * rights + lax.div(inner, lefts) * cols + lax.rem(inner, cols)

    slot_count = cols_ref.shape[1]
    ids = [cols_ref[0, s] for s in range(slot_count)]
    live_slots = live_ref[0, 0]
    left_parts = [lax.rem(lax.div(k, cols), depths) for k in ids]
    right_parts = [lax.div(k, rows * depths) for k in ids]
    lane = lax.broadcasted_iota(jnp.int32, index_row.shape, 1)
    wide = lax.broadcasted_iota(jnp.int32, meta_ref.shape[1:], 1)
    index = jnp.zeros(index_row.shape, jnp.int32)
    table = jnp.zeros(meta_ref.shape[1:], jnp.int32)
    for s in range(slot_count):
        left_rank, right_rank = jnp.int32(0), jnp.int32(0)
        for before in range(s):
            left_rank += jnp.where(left_parts[before] == left_parts[s], 1, 0)
            right_rank += jnp.where(right_parts[before] == right_parts[s], 1, 0)
        live = s < live_slots
        left_to = jnp.where(live, left_parts[s] * cap_left + left_rank, -1)
        right_to = jnp.where(live, left_total + right_parts[s] * cap_right + right_rank, -1)
        index = jnp.where((lane == left_to) | (lane == right_to), s, index)
        code = left_rank + 1 + 256 * (right_rank + 1)
        table = jnp.where(wide == jnp.where(live, placed(ids[s]), -1), code, table)
    index_row[...] = index
    meta_ref[0] = table
    index_copy = pltpu.make_async_copy(index_row, index_ref, local_sems.at[3])
    index_copy.start()
    index_copy.wait()

    values_copy.wait()
    for at, (turn, flip) in enumerate(turns):
        cc = column(turn, flip)
        for q in range(cap_right):
            block = values_ref[index_ref[0, left_total + cc * cap_right + q]]
            if at == 0:
                planes[0][q] = block
            else:
                right_stage[at - 1, q] = block
    left_meta[left_me] = meta_ref[0]
    right_meta[right_me] = meta_ref[0]
    for plane in planes:
        plane[zero_slot] = jnp.zeros(plane.shape[1:], plane.dtype)

    pl.semaphore_wait(barrier, len(greeted))

    def hops(rr, rank):
        plane = ranked[rr][rank]
        for step, ahead in ((1, plane <= rr < rows - 1), (-1, plane >= rr > 0)):
            if ahead:
                yield step, ranked[rr + step].index(plane)

    def line(rank, at):
        def run(rr):
            for step, there in hops(rr, rank):
                remote(
                    chunk(rank, at),
                    chunk(there, at),
                    line_send.at[(step + 1) // 2, rank, at],
                    right_sem.at[there, at],
                    (r + step, c, d),
                )

        for rr in range(rows):
            if list(hops(rr, rank)):
                pl.when(r == rr)(functools.partial(run, rr))

    line(0, 0)
    for at in [*range(1, cols - 1), 0]:
        turn, flip = turns[at + 1]
        remote(
            right_stage.at[at],
            chunk(0, at + 1),
            right_send.at[at],
            right_sem.at[0, at + 1],
            (r, column(turn, flip), d),
        )
    for e in range(depths):
        dd = lax.rem(d + e, depths)
        for q in range(cap_left):
            block = values_ref[index_ref[0, dd * cap_left + q]]
            if e == 0:
                left_buf[left_me * cap_left + q] = block
            else:
                left_stage[e - 1, q] = block

    def pass_left(source):
        return remote(
            left_chunk(source),
            left_chunk(source),
            pass_send.at[source],
            left_sem.at[source],
            (r, other_core, d),
        )

    def send_left(some):
        for e in range(depths):
            for turn in some:
                if turn or e:
                    remote(
                        left_chunk(left_me) if e == 0 else left_stage.at[e - 1],
                        left_chunk(left_me),
                        left_send.at[e, turn],
                        left_sem.at[left_me],
                        (r, column(turn, 0), lax.rem(d + e, depths)),
                    )

    send_left(range(1))
    passed = [pass_left(left_me)]

    def take(rank, at):
        wait_all(chunk(rank, at), right_sem.at[rank, at])
        line(rank, at)

    for at in range(1, cols):
        take(0, at)

    send_left(range(1, cols // 2))
    for m, e in left_peers:
        remote(meta_ref, left_meta.at[pl.ds(left_me, 1)], meta_send.at[0], meta_sems.at[0], left_peer(m, e))
    for m, n in right_peers:
        remote(meta_ref, right_meta.at[pl.ds(right_me, 1)], meta_send.at[1], meta_sems.at[1], right_peer(m, n))


    sources = [column(turn, flip, -1) for turn, flip in turns]

    @pl.when(jnp.logical_not(at_end))
    def _():
        for at in range(cols):
            take(1, at)
            take(2, at)

    wait_all(left_meta.at[pl.ds(0, lefts - 1)], meta_sems.at[0])
    wait_all(right_meta.at[pl.ds(0, rights - 1)], meta_sems.at[1])
    left_copy = pltpu.make_async_copy(left_meta, left_ids, local_sems.at[0])
    right_copy = pltpu.make_async_copy(right_meta, right_ids, local_sems.at[1])
    left_copy.start()
    right_copy.start()
    left_copy.wait()
    right_copy.wait()

    slots = []
    for source in range(cols):
        turn = lax.rem(c // 2 + half - source // 2, half)
        slots.append(turn * 2 + jnp.where(lax.rem(c, 2) == source % 2, 0, 1))

    def look_up(p, carry):
        i = lax.rem(pattern_ref[0, p], lefts)
        j = placed(pattern_ref[1, p])
        for inner in range(rights):
            q = lax.rem(left_ids[i, 0, d * rights + inner], 256)
            t = lax.div(right_ids[inner, 0, j], 256)
            slot = slots[inner % cols] * cap_right + t - 1
            right_at[p, inner] = jnp.where((q > 0) & (t > 0), slot, zero_slot)
            left_at[p, inner] = i * cap_left + jnp.maximum(q - 1, 0)
        return carry

    lax.fori_loop(0, depths * share, look_up, 0)

    for e in range(depths):
        for turn in range(cols // 2):
            if turn or e:
                source = lax.rem(d + depths - e, depths) * cols + column(turn, 0, -1)
                wait_all(left_chunk(source), left_sem.at[source])
                passed.append(pass_left(source))

    @pl.when(jnp.logical_not(at_end))
    def _():
        for at in range(cols):
            take(rows - 1, at)

    for e in range(depths):
        for turn in range(cols // 2):
            source = lax.rem(d + depths - e, depths) * cols + column(turn, 1, -1)
            wait_all(left_chunk(source), left_sem.at[source])

    def add_plane(rank, first, count, ats=range(cols), last=False, mine=False):
        plane = jnp.int32(0)
        for rr in range(rows):
            plane = jnp.where(r == rr, ranked[rr][rank], plane)
        held = planes[rows if last else rank]

        def step(u, carry):
            p = first + u
            left_parts, right_parts = [], []
            for at in ats:
                inner = plane * cols + sources[at]
                left_parts.append(left_buf[left_at[p, inner]])
                right_parts.append(held[right_at[p, inner]])
            product = jnp.dot(
                jnp.concatenate(left_parts, axis=1),
                jnp.concatenate(right_parts, axis=0),
                preferred_element_type=jnp.float32,
            )
            if last:
                late_sum[p] += product
                if not mine:
                    late[p] = encode(late_sum[p], bound)
            elif rank == rows - 1:
                late_sum[p] = product
            elif rank == 0:
                partial[p] = product
            else:
                partial[p] += product
            return carry

        lax.fori_loop(0, count, step, 0, unroll=min(count, 4))

    def all_chunks(rank, ats=range(cols)):
        for at in ats:
            wait_all(chunk(rank, at), right_sem.at[rank, at])

    entries = depths * share
    add_plane(0, 0, entries)
    pl.when(at_end)(lambda: all_chunks(1))
    add_plane(1, 0, entries)

    pl.when(at_end)(lambda: all_chunks(2))
    add_plane(2, 0, entries)
    early, final = range(half), range(half, cols)
    copies, late_copies = [], []
    for e in range(1, depths):
        dd = lax.rem(d + e, depths)
        copies.append(
            remote(
                partial.at[pl.ds(dd * share, share)],
                arrived.at[e - 1],
                part_send.at[e - 1],
                part_recv.at[e - 1],
                (r, c, dd),
            )
        )
    pl.when(at_end)(lambda: all_chunks(rows - 1, early))
    add_plane(rows - 1, 0, entries, early)
    pl.when(at_end)(lambda: all_chunks(rows - 1, final))
    pieces = 2 if share % 2 == 0 else 1
    piece = share // pieces
    for e in range(1, depths):
        dd = lax.rem(d + e, depths)
        for h in range(pieces):
            begin = dd * share + h * piece
            add_plane(rows - 1, begin, piece, final, last=True)
            late_copies.append(
                remote(
                    late.at[pl.ds(begin, piece)],
                    late_arrived.at[e - 1, pl.ds(h * piece, piece)],
                    late_send.at[e - 1, h],
                    late_recv.at[e - 1, h],
                    (r, c, dd),
                )
            )
    add_plane(rows - 1, d * share, share, final, last=True, mine=True)
    total = partial[pl.ds(d * share, share)] + late_sum[pl.ds(d * share, share)]
    for e, copy in enumerate(copies):
        copy.wait_recv()
        total = total + arrived[e]
    for copy in late_copies:
        copy.wait_recv()
    for e in range(depths - 1):
        total = total + decode(late_arrived[e], bound)
    out_ref[...] = jnp.log1p(total).astype(out_ref.dtype)

    for copy in copies + late_copies + passed:
        copy.wait_send()

    def line_sent(rr):
        for rank in range(rows):
            for step, there in hops(rr, rank):
                for at in range(cols):
                    wait_all(chunk(rank, at), line_send.at[(step + 1) // 2, rank, at])

    for rr in range(rows):
        pl.when(r == rr)(functools.partial(line_sent, rr))
    for at in range(cols - 1):
        wait_all(right_stage.at[at], right_send.at[at])
    for e in range(depths):
        for turn in range(cols // 2):
            if turn or e:
                wait_all(left_chunk(left_me), left_send.at[e, turn])
    wait_all(left_meta.at[pl.ds(0, lefts - 1)], meta_send.at[0])
    wait_all(right_meta.at[pl.ds(0, rights - 1)], meta_send.at[1])


def body(block_values, block_cols, live_count, out_pattern):
    depths = lax.axis_size("depth")
    cols = lax.axis_size("col")
    rows = lax.axis_size("row")
    slots, size = block_values.shape[2], block_values.shape[3]
    groups = rows * depths
    blocks = groups * cols
    pair = groups // cols
    cap_left = slots // depths
    cap_right = pair * (slots // groups) + min(pair, slots % groups)
    entries = out_pattern.shape[2]
    share = entries // depths
    lefts, rights = cols * depths, rows * cols

    width = -(-blocks // 128) * 128
    pattern = jnp.swapaxes(out_pattern, 2, 3).reshape(2, entries)

    block = (size, size)
    bf16, i32 = jnp.bfloat16, jnp.int32
    vmem, smem = pltpu.VMEM, pltpu.SMEM
    dma = pltpu.SemaphoreType.DMA
    result = pl.pallas_call(
        functools.partial(kernel, (rows, cols, depths, cap_left, cap_right)),
        out_shape=jax.ShapeDtypeStruct((share,) + block, bf16),
        in_specs=[
            pl.BlockSpec(memory_space=smem),
            pl.BlockSpec(memory_space=smem),
            pl.BlockSpec(memory_space=smem),
            pl.BlockSpec(memory_space=pl.ANY),
        ],
        out_specs=pl.BlockSpec(memory_space=vmem),
        scratch_shapes=[
            vmem((slots,) + block, bf16),
            vmem((1, 128), i32),
            smem((1, 128), i32),
            vmem((1, 1, width), i32),
            vmem((depths - 1, cap_left) + block, bf16),
            vmem((cols - 1, cap_right) + block, bf16),
            vmem((lefts * cap_left,) + block, bf16),
            vmem((lefts, 1, width), i32),
            vmem((rights, 1, width), i32),
            smem((lefts, 1, width), i32),
            smem((rights, 1, width), i32),
            smem((entries, rights), i32),
            smem((entries, rights), i32),
            vmem((entries,) + block, jnp.float32),
            vmem((entries,) + block, LATE),
            vmem((entries,) + block, jnp.float32),
            vmem((depths - 1, share) + block, jnp.float32),
            vmem((depths - 1, share) + block, LATE),
            dma((depths, cols // 2)),
            dma((lefts,)),
            dma((lefts,)),
            dma((cols - 1,)),
            dma((rows, cols)),
            dma((2, rows, cols)),
            dma((2,)),
            dma((2,)),
            dma((4,)),
            dma((depths - 1,)),
            dma((depths - 1,)),
            dma((depths - 1, 2)),
            dma((depths - 1, 2)),
        ]
        + [vmem((cols * cap_right + 1,) + block, bf16)] * (rows + 1),
        compiler_params=pltpu.CompilerParams(
            collective_id=0, has_side_effects=True, vmem_limit_bytes=56 * 1024 * 1024
        ),
    )(block_cols.reshape(1, slots), live_count, pattern, block_values.reshape((slots,) + block))
    return result.reshape((1, 1, share) + block)


def solution(mesh):
    in_specs = (
        P(("row", "depth"), "col", None, None, None),
        P(("row", "depth"), "col", None),
        P(("row", "depth"), "col"),
        P("row", "col", None, None),
    )
    out_specs = P("row", "col", "depth", None, None)
    return jax.shard_map(body, mesh=mesh, in_specs=in_specs, out_specs=out_specs, check_vma=False)
```
